256 devices in a mesh: grp: 16 (over z_hi, y), resp: 16 (over z_lo, x, core).
Axes of the slice: x: 4, y: 4, z: 8 (z_hi: 4, z_lo: 2; z = z_hi * 2 + z_lo), core: 2. Of those that a mesh axis runs over, the one named last changes fastest.
Arguments:
- prompt_kv: bfloat16 [32768, 2, 512], P(('grp', 'resp')), parts along dimension 0, may hold values from -4 to 4
- queries: bfloat16 [32768, 2560], P(('grp', 'resp')), parts along dimension 0, may hold values from -100 to 100, as said below
- response_key_values: bfloat16 [32768, 2, 512], P(('grp', 'resp')), parts along dimension 0, may hold values from -4 to 4
- grad_out: bfloat16 [32768, 2560], P(('grp', 'resp')), parts along dimension 0, may hold values from -6 to 6
- lengths: int32 [256], P(('grp', 'resp')), parts along dimension 0, may hold values from 1 to 128, 1536 in all
Outputs:
- attn_out: bfloat16 [32768, 2560], P(('grp', 'resp')), parts along dimension 0
- grad_queries: bfloat16 [32768, 2560], P(('grp', 'resp')), parts along dimension 0
- grad_resp_kv: bfloat16 [32768, 2, 512], P(('grp', 'resp')), parts along dimension 0
- grad_prompt_kv: bfloat16 [32768, 2, 512], P(('grp', 'resp')), parts along dimension 0
The draws below stay inside these ranges and needn't reach their ends.
There are 16 independent parts, one for each index of `grp`. The reference program is written for one: setup_inputs(seed, part) draws one part's arguments, and reference() takes and returns one part's arrays. A program takes and returns all parts, laid end to end along the dimension named above; each array names one. Nothing has to cross between parts.
Inputs may be any that keep to these rules, and one draw needn't show every extreme that they name: `lengths`: every response has at least one live token, and in each prompt's batch the longest response fills all 128 slots. `queries`: queries after their rotary position.
All inputs are finite; a program needn't handle non-finite values. No bound on the sum of `lengths` on one device may be relied on, other than what follows from the above.
Results may differ from the reference program's by a relative error of at most 0.024.
Values may be sent and summed in bfloat16 or wider, within the bound.
A program may use at most 128 MiB of HBM per device.

```python
import math
import jax
import jax.numpy as jnp
import numpy as np
from jax import lax

QUERY_HEADS = 20
KEY_VALUE_HEADS = 4
HEAD_SIZE = 128
RESPONSE_SLOTS = 128
PROMPT_LENGTH = 2048
RESPS = 16
RESPONSE_TOKENS = 2048


def shared_keys(key):
    return jnp.clip(jax.random.normal(key, (PROMPT_LENGTH, 2, KEY_VALUE_HEADS * HEAD_SIZE), jnp.float32), -4.0, 4.0)


def draw_prompt_kv(key, part):
    base_offset = shared_keys(key)
    return base_offset.astype(jnp.bfloat16)


def draw_queries(key, part):
    key = jax.random.fold_in(key, 23)
    key_noise = jax.random.fold_in(key, 0)
    total_width = QUERY_HEADS * HEAD_SIZE
    drawn = jnp.clip(jax.random.normal(key_noise, (RESPONSE_TOKENS, total_width), jnp.float32), -5.0, 5.0)
    return drawn.astype(jnp.bfloat16)


def block_levels(stream_key, extent, pieces, least, top_value):
    level, own = 1.0, jax.random.fold_in(stream_key, 6)
    for axis_at, blocks in pieces:
        heights = jnp.exp(jax.random.uniform(jax.random.fold_in(own, axis_at), (blocks,), jnp.float32, least / len(pieces), top_value / len(pieces)))
        level = level * jnp.repeat(heights, extent[axis_at] // blocks).reshape([-1 if axis == axis_at else 1 for axis in range(len(extent))])
    return level


def profile(count, total, bound, lean):
    weights = [(1 << 20) // math.isqrt(standing ** lean) + 1 for standing in range(2, count + 1)]
    rest, given = total - bound - (count - 1), [1] * (count - 1)
    while rest > 0:
        free = [i for i in range(count - 1) if given[i] < bound]
        mass, remaining = sum([weights[i] for i in free]), rest
        for i in free:
            addition = min(bound - given[i], max(1, remaining * weights[i] // mass), rest)
            given[i] = given[i] + addition
            rest = rest - addition
    return np.array([bound] + given)


def ragged_sizes(rng, number_of, total, reach, slope):
    if number_of == 2:
        one = jax.random.randint(rng, (), max(1, total - reach), min(reach, total - 1) + 1)
        return jnp.stack([one, total - one])
    tallies = jnp.asarray(profile(number_of, total, reach, slope), jnp.int32)
    couples = (number_of - 1) // 2
    donor, receiver = tallies[1:1 + 2 * couples:2], tallies[2:2 + 2 * couples:2]
    room = jnp.minimum(donor - 1, reach - receiver)
    moved = jax.random.randint(jax.random.fold_in(rng, 1), (couples,), 0, 1 << 20) % (room + 1)
    tallies = tallies.at[1:1 + 2 * couples:2].set(donor - moved).at[2:2 + 2 * couples:2].set(receiver + moved)
    return tallies[jax.random.permutation(jax.random.fold_in(rng, 2), number_of)]


def bell_draw(stream_key, extent, scale, reach, cuts=(), kind=jnp.bfloat16):
    result = jax.random.normal(stream_key, extent, jnp.float32) * scale
    if len(cuts) > 0:
        result = block_levels(stream_key, extent, cuts, -0.22, 0.18) * result
    return jnp.clip(result, min=-reach, max=reach).astype(kind)


def setup_inputs(seed: int = 0, part: int = 0) -> dict:
    key_of = jax.random.split(jax.random.key(seed), 6)
    part_splits = jax.random.split(jax.random.fold_in(key_of[5], part), 6)
    return {
        "prompt_kv": draw_prompt_kv(jax.random.fold_in(jax.random.fold_in(key_of[5], part), 71), part),
        "queries": draw_queries(jax.random.fold_in(jax.random.fold_in(key_of[5], part), 71), part),
        "response_key_values": bell_draw(part_splits[2], (RESPONSE_TOKENS, 2, KEY_VALUE_HEADS * HEAD_SIZE), 1.0, 4.0, ((0, 16),)),
        "grad_out": bell_draw(part_splits[3], (RESPONSE_TOKENS, QUERY_HEADS * HEAD_SIZE), 1.0, 6.0, ((0, 16),)),
        "lengths": ragged_sizes(part_splits[4], RESPS, 3 * RESPONSE_SLOTS * RESPS // 4, RESPONSE_SLOTS, 1).astype(jnp.int32),
    }


MASKED_SCORE = -1e+30

def head_pass(head_query, head_keys, head_values, head_grad, visible):
    inv_root = 1.0 / math.sqrt(HEAD_SIZE)
    query_wide = head_query.astype(jnp.float32)
    keys_wide = head_keys.astype(jnp.float32)
    values_wide = head_values.astype(jnp.float32)
    grad_wide = head_grad.astype(jnp.float32)
    scores = jnp.einsum('rgd,ld->grl', query_wide, keys_wide) * inv_root
    scores = jnp.where(visible[None], scores, MASKED_SCORE)
    row_max = lax.optimization_barrier(jnp.max(scores, axis=-1, keepdims=True))
    raised = jnp.exp(scores - row_max)
    weights = raised / lax.optimization_barrier(jnp.sum(raised, axis=-1, keepdims=True))
    weights_low = weights.astype(jnp.bfloat16)
    attended = jnp.einsum('grl,ld->rgd', weights_low.astype(jnp.float32), values_wide)
    dweights = jnp.einsum('rgd,ld->grl', grad_wide, values_wide)
    row_delta = jnp.einsum('rgd,rgd->gr', grad_wide, attended)[..., None]
    dscore_low = (weights * (dweights - row_delta)).astype(jnp.bfloat16)
    dscore_wide = dscore_low.astype(jnp.float32)
    grad_query = jnp.einsum('grl,ld->rgd', dscore_wide, keys_wide) * inv_root
    grad_keys = jnp.einsum('grl,rgd->ld', dscore_wide, query_wide) * inv_root
    grad_values = jnp.einsum('grl,rgd->ld', weights_low.astype(jnp.float32), grad_wide)
    return (attended, grad_query, grad_keys, grad_values)

def reference(prompt_kv, queries, response_key_values, grad_out, lengths):
    key_value_width = KEY_VALUE_HEADS * HEAD_SIZE
    group_width = QUERY_HEADS // KEY_VALUE_HEADS
    positions = jnp.arange(RESPONSE_SLOTS, dtype=jnp.int32)
    causal = positions[:, None] >= positions[None, :]
    visible = jnp.concatenate([jnp.full((RESPONSE_SLOTS, PROMPT_LENGTH), True), causal], axis=1)

    def one_response(summed, resp_index):
        starting_row = (resp_index * RESPONSE_SLOTS).astype(jnp.int32)
        query_block = lax.dynamic_slice_in_dim(queries, starting_row, RESPONSE_SLOTS, 0).reshape(RESPONSE_SLOTS, KEY_VALUE_HEADS, group_width, HEAD_SIZE)
        own_kv = lax.dynamic_slice_in_dim(response_key_values, starting_row, RESPONSE_SLOTS, 0)
        row_gradients = lax.dynamic_slice_in_dim(grad_out, starting_row, RESPONSE_SLOTS, 0)
        is_valid = positions < lengths[resp_index]
        row_gradients = jnp.where(is_valid[:, None], row_gradients, jnp.zeros_like(row_gradients))
        head_gradients = row_gradients.reshape(RESPONSE_SLOTS, KEY_VALUE_HEADS, group_width, HEAD_SIZE)
        attended_list, query_list, key_list, value_list = ([], [], [], [])
        for key_value_head in range(KEY_VALUE_HEADS):
            columns = slice(key_value_head * HEAD_SIZE, (key_value_head + 1) * HEAD_SIZE)
            head_keys = jnp.concatenate([prompt_kv[:, 0, columns], own_kv[:, 0, columns]], axis=0)
            head_values = jnp.concatenate([prompt_kv[:, 1, columns], own_kv[:, 1, columns]], axis=0)
            attended, grad_query, grad_keys, grad_values = head_pass(query_block[:, key_value_head], head_keys, head_values, head_gradients[:, key_value_head], visible)
            attended_list.append(attended)
            query_list.append(grad_query)
            key_list.append(grad_keys)
            value_list.append(grad_values)
        attended = jnp.stack(attended_list, axis=1).reshape(RESPONSE_SLOTS, QUERY_HEADS * HEAD_SIZE)
        out_rows = jnp.where(is_valid[:, None], attended, 0.0).astype(jnp.bfloat16)
        query_grad = jnp.stack(query_list, axis=1).reshape(RESPONSE_SLOTS, QUERY_HEADS * HEAD_SIZE).astype(jnp.bfloat16)
        key_grad = jnp.concatenate(key_list, axis=1)
        value_grad = jnp.concatenate(value_list, axis=1)
        own_grad = jnp.stack([key_grad[PROMPT_LENGTH:], value_grad[PROMPT_LENGTH:]], axis=1).astype(jnp.bfloat16)
        prompt_term = jnp.stack([key_grad[:PROMPT_LENGTH], value_grad[:PROMPT_LENGTH]], axis=1)
        prompt_partial = lax.optimization_barrier(prompt_term.astype(jnp.bfloat16))
        return (summed + prompt_partial.astype(jnp.float32), (out_rows, query_grad, own_grad))
    initial = jnp.zeros((PROMPT_LENGTH, 2, key_value_width), jnp.float32)
    summed, stacked = lax.scan(one_response, initial, jnp.arange(RESPS, dtype=jnp.int32))
    attn_out = stacked[0].reshape(RESPONSE_TOKENS, QUERY_HEADS * HEAD_SIZE)
    grad_queries = stacked[1].reshape(RESPONSE_TOKENS, QUERY_HEADS * HEAD_SIZE)
    grad_resp_kv = stacked[2].reshape(RESPONSE_TOKENS, 2, key_value_width)
    return (attn_out, grad_queries, grad_resp_kv, summed.astype(jnp.bfloat16))
```

```python
import functools
import math

import jax
import jax.numpy as jnp
from jax import lax
from jax.experimental import pallas as pl
from jax.experimental.pallas import tpu as pltpu
from jax.sharding import PartitionSpec as P

D = 128
T = 128
G = 5
KVH = 4
BLK = 2 * T
COLS = G * T
R = 2 * COLS
NP = 8
MASKED = -1e30
INV_ROOT = 1.0 / math.sqrt(D)
SCALE2 = INV_ROOT * math.log2(math.e)
BF = jnp.bfloat16
F32 = jnp.float32
MESH = pl.DeviceIdType.MESH


def dot(a, b, ca, cb):
    return lax.dot_general(a, b, (((ca,), (cb,)), ((), ())), preferred_element_type=F32)


def kernel(pkv, pack, oout, qout, rout, pout,
           kvb, xb, sb, srb, eb, erb, mb, lb, ot, gp, dlt, dqt, osend, qsend, rsend, pb, rb, fsend,
           st_s, st_r, loc, ag_s, ag_r, rs_s, rs_r, out_s, out_r):
    me = lax.axis_index("resp")
    z, x, c = me // 8, (me // 2) % 4, me % 2
    XP = z * 8 + ((x + 1) % 4) * 2 + c
    XM = z * 8 + ((x + 3) % 4) * 2 + c
    ZP = (1 - z) * 8 + x * 2 + c
    SIB = z * 8 + x * 2 + (1 - c)

    def remote(src, dst, ss, rs, to):
        return pltpu.make_async_remote_copy(
            src_ref=src, dst_ref=dst, send_sem=ss, recv_sem=rs, device_id={"resp": to}, device_id_type=MESH)

    barrier = pltpu.get_barrier_semaphore()
    for to in (XP, XM, ZP, SIB):
        pl.semaphore_signal(barrier, inc=1, device_id={"resp": to}, device_id_type=MESH)
    pl.semaphore_wait(barrier, 4)

    mine, other = 2 * c, 2 * (1 - c)
    rows = pl.ds(pl.multiple_of(c * T, T), T)
    orows = pl.ds(pl.multiple_of((1 - c) * T, T), T)
    ex_kv = remote(pkv.at[pl.ds(other, 2)], kvb.at[:, 0, :, rows, :], st_s.at[0], st_r.at[0], SIB)
    ex_kv.start()
    own_kv = pltpu.make_async_copy(pkv.at[pl.ds(mine, 2)], kvb.at[:, 0, :, rows, :], loc.at[0])
    own_kv.start()
    ex_x = remote(pack.at[pl.ds(other, 2)], xb.at[:, 1], st_s.at[1], st_r.at[1], SIB)
    ex_x.start()
    own_x = pltpu.make_async_copy(pack.at[pl.ds(mine, 2)], xb.at[:, 0], loc.at[1])
    own_x.start()

    def ag(a, kv, kind):
        to = (XP, XM, ZP, XP, XM, XP, XM, ZP)[kind]
        src = (0, 0, 0, 3, 3, 1, 2, 6)[kind]
        dst = (1, 2, 3, 4, 5, 6, 6, 7)[kind]
        part = {5: pl.ds(0, T), 6: pl.ds(T, T)}.get(kind, pl.ds(0, BLK))
        return remote(kvb.at[a, src, kv, part, :], kvb.at[a, dst, kv, part, :],
                      ag_s.at[a, kv, kind], ag_r.at[a, kv, kind], to)

    def ag_first(a, kv):
        for k in (0, 1, 2):
            ag(a, kv, k).start()

    def ag_second(a, kv):
        ag(a, kv, 0).wait_recv()
        ag(a, kv, 5).start()
        ag(a, kv, 1).wait_recv()
        ag(a, kv, 6).start()
        ag(a, kv, 2).wait_recv()
        ag(a, kv, 3).start()
        ag(a, kv, 4).start()

    def ag_third(a, kv):
        ag(a, kv, 5).wait_recv()
        ag(a, kv, 6).wait_recv()
        ag(a, kv, 7).start()

    def ag_wait(a, kv, *kinds):
        for k in kinds:
            ag(a, kv, k).wait_recv()

    def rs(a, kind):
        to = (XM, XP, ZP, XM, XP, XM, XP, ZP)[kind]
        src = (1, 2, 3, 4, 5, 6, 6, 7)[kind]
        part = {5: pl.ds(0, T), 6: pl.ds(T, T)}.get(kind, pl.ds(0, BLK))
        return remote(pb.at[a, src, :, part, :], rb.at[a, kind, :, part, :],
                      rs_s.at[a, kind], rs_r.at[a, kind], to)

    def rs_six(a):
        rs(a, 7).wait_recv()
        pb[a, 6] = (pb[a, 6].astype(F32) + rb[a, 7].astype(F32)).astype(BF)
        rs(a, 5).start()
        rs(a, 6).start()

    def rs_three(a):
        rs(a, 3).wait_recv()
        rs(a, 4).wait_recv()
        pb[a, 3] = (pb[a, 3].astype(F32) + rb[a, 3].astype(F32) + rb[a, 4].astype(F32)).astype(BF)
        rs(a, 2).start()

    def rs_one_two(a):
        rs(a, 5).wait_recv()
        pb[a, 1, :, :T] = (pb[a, 1, :, :T].astype(F32) + rb[a, 5, :, :T].astype(F32)).astype(BF)
        rs(a, 0).start()
        rs(a, 6).wait_recv()
        pb[a, 2, :, T:] = (pb[a, 2, :, T:].astype(F32) + rb[a, 6, :, T:].astype(F32)).astype(BF)
        rs(a, 1).start()

    def p_copy(a):
        return remote(fsend.at[a], pout.at[2 * c + a], out_s.at[a, 3], out_r.at[a, 3], SIB)

    def rs_final(a):
        for k in (0, 1, 2):
            rs(a, k).wait_recv()

        def total(part):
            return (pb[a, 0, :, part, :].astype(F32) + rb[a, 0, :, part, :].astype(F32)
                    + rb[a, 1, :, part, :].astype(F32) + rb[a, 2, :, part, :].astype(F32)).astype(BF)

        fsend[a] = total(orows)
        p_copy(a).start()
        pout[2 * c + a] = total(rows)

    def o_copy(a):
        return remote(osend.at[a], oout.at[pl.ds((2 * c + a) * G, G)], out_s.at[a, 0], out_r.at[a, 0], SIB)

    def q_copy(a):
        return remote(qsend.at[a], qout.at[pl.ds((2 * c + a) * G, G)], out_s.at[a, 1], out_r.at[a, 1], SIB)

    def r_copy(a):
        return remote(rsend.at[a], rout.at[2 * c + a], out_s.at[a, 2], out_r.at[a, 2], SIB)

    def at_step(i, hooks):
        for k, calls in hooks.items():
            @pl.when(i == k)
            def _():
                for call in calls:
                    call()

    def queries_of(a):
        return jnp.concatenate([xb[a, b, 0:G].reshape(COLS, D) for b in (0, 1)], axis=0)

    def fold(value, op):
        n = value.shape[0]
        return op(value.reshape(n // 8, 8, R), axis=0)

    def head(a, hooks_a, hooks_b, hooks_c, ends_c):
        slot = lax.broadcasted_iota(jnp.int32, (T, G, T), 2).reshape(T, COLS)
        key = lax.broadcasted_iota(jnp.int32, (T, COLS), 0)
        for b in (0, 1):
            s = dot(xb[a, b, 2 * G], xb[a, b, 0:G].reshape(COLS, D), 1, 1)
            srb[:, b * COLS:(b + 1) * COLS] = jnp.where(key <= slot, s, MASKED)
        mb[...] = fold(srb[...], jnp.max)

        def score_step(p, _):
            at_step(p, hooks_a)
            s = dot(kvb[a, p, 0], queries_of(a), 1, 1)
            sb[p] = s
            mb[...] = jnp.maximum(mb[...], fold(s, jnp.max))
            return 0

        lax.fori_loop(0, NP, score_step, 0)

        top = jnp.max(mb[...], axis=0, keepdims=True) * SCALE2
        mb[0:1] = top
        er = jnp.exp2(srb[...] * SCALE2 - top)
        lb[...] = fold(er, jnp.sum)
        erb[...] = er.astype(BF)
        for b in (0, 1):
            cols = slice(b * COLS, (b + 1) * COLS)
            ot[:, cols] = dot(xb[a, b, 2 * G + 1], erb[:, cols], 0, 0)

        def weight_step(p, _):
            at_step(p, hooks_b)
            e = jnp.exp2(sb[p] * SCALE2 - mb[0:1])
            lb[...] += fold(e, jnp.sum)
            low = e.astype(BF)
            eb[p] = low
            ot[...] += dot(kvb[a, p, 1], low, 0, 0)
            return 0

        lax.fori_loop(0, NP, weight_step, 0)

        inv = 1.0 / jnp.sum(lb[...], axis=0, keepdims=True)
        for b in (0, 1):
            for g in range(G):
                lo = b * COLS + g * T
                cols = slice(lo, lo + T)
                att = ot[:, cols] * inv[:, cols]
                gt = xb[a, b, G + g].astype(F32).T
                dlt[:, cols] = jnp.sum(gt * att, axis=0, keepdims=True) * inv[:, cols]
                gp[cols, :] = (gt * inv[:, cols]).T.astype(BF)
                if b == 0:
                    oout[(2 * c + a) * G + g] = att.T.astype(BF)
                else:
                    osend[a, g] = att.T.astype(BF)
        o_copy(a).start()

        for b in (0, 1):
            cols = slice(b * COLS, (b + 1) * COLS)
            dp = dot(xb[a, b, 2 * G + 1], gp[cols, :], 1, 1) - dlt[:, cols]
            ds = (erb[:, cols].astype(F32) * dp).astype(BF)
            dv = dot(erb[:, cols], gp[cols, :], 1, 0).astype(BF)
            dk = (dot(ds, xb[a, b, 0:G].reshape(COLS, D), 1, 0) * INV_ROOT).astype(BF)
            dqt[:, cols] = dot(xb[a, b, 2 * G], ds, 0, 0)
            if b == 0:
                rout[2 * c + a, 0] = dk
                rout[2 * c + a, 1] = dv
            else:
                rsend[a, 0] = dk
                rsend[a, 1] = dv
        r_copy(a).start()

        def grad_step(i, _):
            at_step(i, hooks_c)
            p = NP - 1 - i
            dp = dot(kvb[a, p, 1], gp[...], 1, 1) - dlt[...]
            ds = (eb[p].astype(F32) * dp).astype(BF)
            pb[a, p, 1] = dot(eb[p], gp[...], 1, 0).astype(BF)
            pb[a, p, 0] = (dot(ds, queries_of(a), 1, 0) * INV_ROOT).astype(BF)
            dqt[...] += dot(kvb[a, p, 0], ds, 0, 0)
            at_step(i, ends_c)
            return 0

        lax.fori_loop(0, NP, grad_step, 0)
        for b in (0, 1):
            for g in range(G):
                lo = b * COLS + g * T
                grad = (dqt[:, lo:lo + T] * INV_ROOT).T.astype(BF)
                if b == 0:
                    qout[(2 * c + a) * G + g] = grad
                else:
                    qsend[a, g] = grad
        q_copy(a).start()

    f = functools.partial
    ex_kv.wait_recv()
    own_kv.wait()
    ag_first(0, 0)
    ag_first(0, 1)
    ex_x.wait_recv()
    own_x.wait()

    ends_c = lambda a: {0: [rs(a, 7).start], 2: [rs(a, 4).start], 3: [rs(a, 3).start, f(rs_six, a)]}
    head(0,
         {1: [f(ag_second, 0, 0), f(ag_first, 1, 0)],
          4: [f(ag_third, 0, 0), f(ag_second, 0, 1), f(ag_first, 1, 1), f(ag_wait, 0, 0, 3, 4)],
          7: [f(ag_wait, 0, 0, 7)]},
         {0: [f(ag_third, 0, 1), f(ag_second, 1, 0)],
          4: [f(ag_wait, 0, 1, 3, 4)],
          7: [f(ag_third, 1, 0), f(ag_second, 1, 1), f(ag_wait, 0, 1, 7)]},
         {2: [f(ag_third, 1, 1)]},
         ends_c(0))
    head(1,
         {0: [f(ag_wait, 1, 0, 3, 4)],
          2: [f(rs_three, 0), f(rs_one_two, 0)],
          7: [f(ag_wait, 1, 0, 7)]},
         {0: [f(ag_wait, 1, 1, 3, 4)],
          7: [f(ag_wait, 1, 1, 7)]},
         {0: [f(rs_final, 0)]},
         ends_c(1))
    rs_three(1)
    rs_one_two(1)
    rs_final(1)

    ex_kv.wait_send()
    ex_x.wait_send()
    for a in (0, 1):
        for kind in range(8):
            ag(a, 0, kind).wait_send()
            ag(a, 1, kind).wait_send()
            rs(a, kind).wait_send()
        for copy in (o_copy(a), q_copy(a), r_copy(a), p_copy(a)):
            copy.wait()


def per_device(prompt_kv, queries, response_key_values, grad_out, lengths):
    live = (jnp.arange(T, dtype=jnp.int32) < lengths[0])[:, None]
    grads = jnp.where(live, grad_out, jnp.zeros_like(grad_out))
    pkv = prompt_kv.reshape(T, 2, KVH, D).transpose(2, 1, 0, 3)
    rkv = response_key_values.reshape(T, 2, KVH, D).transpose(2, 1, 0, 3)
    by_head = lambda v: v.reshape(T, KVH, G, D).transpose(1, 2, 0, 3)
    pack = jnp.concatenate([by_head(queries), by_head(grads), rkv], axis=1)
    vmem = pl.BlockSpec(memory_space=pltpu.VMEM)
    dma = pltpu.SemaphoreType.DMA
    flops = 6 * 2 * 2 * R * (NP * BLK + T) * D
    oout, qout, rout, pout = pl.pallas_call(
        kernel,
        out_shape=(
            jax.ShapeDtypeStruct((KVH * G, T, D), BF),
            jax.ShapeDtypeStruct((KVH * G, T, D), BF),
            jax.ShapeDtypeStruct((KVH, 2, T, D), BF),
            jax.ShapeDtypeStruct((KVH, 2, T, D), BF),
        ),
        in_specs=[vmem, vmem],
        out_specs=(vmem,) * 4,
        scratch_shapes=[
            pltpu.VMEM((2, NP, 2, BLK, D), BF),
            pltpu.VMEM((2, 2, 2 * G + 2, T, D), BF),
            pltpu.VMEM((NP, BLK, R), F32),
            pltpu.VMEM((T, R), F32),
            pltpu.VMEM((NP, BLK, R), BF),
            pltpu.VMEM((T, R), BF),
            pltpu.VMEM((8, R), F32),
            pltpu.VMEM((8, R), F32),
            pltpu.VMEM((D, R), F32),
            pltpu.VMEM((R, D), BF),
            pltpu.VMEM((1, R), F32),
            pltpu.VMEM((D, R), F32),
            pltpu.VMEM((2, G, T, D), BF),
            pltpu.VMEM((2, G, T, D), BF),
            pltpu.VMEM((2, 2, T, D), BF),
            pltpu.VMEM((2, NP, 2, BLK, D), BF),
            pltpu.VMEM((2, NP, 2, BLK, D), BF),
            pltpu.VMEM((2, 2, T, D), BF),
            dma((2,)), dma((2,)), dma((2,)),
            dma((2, 2, 8)), dma((2, 2, 8)),
            dma((2, 8)), dma((2, 8)),
            dma((2, 4)), dma((2, 4)),
        ],
        compiler_params=pltpu.CompilerParams(
            collective_id=0, has_side_effects=True, vmem_limit_bytes=56 << 20),
        cost_estimate=pl.CostEstimate(flops=flops, bytes_accessed=8 << 20, transcendentals=2 * R * (NP * BLK + T)),
        name="shared_prompt_attention",
    )(pkv, pack)
    flat = lambda v: v.transpose(1, 0, 2).reshape(T, KVH * G * D)
    attn_out = jnp.where(live, flat(oout), jnp.zeros((), BF))
    rows = lambda v: v.transpose(2, 1, 0, 3).reshape(T, 2, KVH * D)
    return attn_out, flat(qout), rows(rout), rows(pout)


def solution(mesh):
    wide, thick = P(("grp", "resp"), None), P(("grp", "resp"), None, None)
    return jax.shard_map(
        per_device,
        mesh=mesh,
        in_specs=(thick, wide, thick, wide, P(("grp", "resp"))),
        out_specs=(wide, wide, thick, thick),
        check_vma=False,
    )
```

```python
import functools
import math

import jax
import jax.numpy as jnp
from jax import lax
from jax.experimental import pallas as pl
from jax.experimental.pallas import tpu as pltpu
from jax.sharding import PartitionSpec as P

D = 128
T = 128
G = 5
KVH = 4
BLK = 2 * T
COLS = G * T
R = 2 * COLS
NP = 8
MASKED = -1e30
INV_ROOT = 1.0 / math.sqrt(D)
SCALE2 = INV_ROOT * math.log2(math.e)
BF = jnp.bfloat16
F32 = jnp.float32
MESH = pl.DeviceIdType.MESH


def dot(a, b, ca, cb):
    return lax.dot_general(a, b, (((ca,), (cb,)), ((), ())), preferred_element_type=F32)


STEP = 2
NI = NP // STEP
N = STEP * BLK
HALF = NI // 2
BACK = (0, 2, 1, 3, 5, 4, 6, 7)
LAST = {0: 0, 1: 1, 2: 2, 3: 3, 7: 4}


def kernel(lengths, prompt, resp, query, grad, oout, qout, rout, pout,
           pkv, rkv, live, kvb, xq, xg, xr, xl, sb, srb, eb, erb, mb, tp, lb, ot, fr, gp, dlt, dqt,
           osend, qsend, rf, rsend, pb, rb, rbf,
           st_s, st_r, loc, d_s, d_r, ag_s, ag_r, rs_s, rs_r, fin_s, fin_r, out_s, out_r):
    me = lax.axis_index("resp")
    z, x, c = me // 8, (me // 2) % 4, me % 2

    def device(p, core):
        dx = (0, 3, 1, 0, 3, 1, 2, 2)[p]
        zz = z if p in (0, 1, 2, 6) else 1 - z
        cc = c if core == 0 else 1 - c
        return zz * 8 + ((x + dx) % 4) * 2 + cc

    def remote(src, dst, ss, rs, to):
        return pltpu.make_async_remote_copy(
            src_ref=src, dst_ref=dst, send_sem=ss, recv_sem=rs, device_id={"resp": to}, device_id_type=MESH)

    barrier = pltpu.get_barrier_semaphore()
    peers = [(p, core) for p in (0, 1, 2, 3, 7) for core in (0, 1) if p or core]
    for p, core in peers:
        pl.semaphore_signal(barrier, inc=1, device_id={"resp": device(p, core)}, device_id_type=MESH)

    sib = device(0, 1)
    mine, other = 2 * c, 2 * (1 - c)
    rows = pl.ds(pl.multiple_of(c * T, T), T)
    orows = pl.ds(pl.multiple_of((1 - c) * T, T), T)
    W = 2 * G * D

    def columns(which):
        return pl.ds(pl.multiple_of(which * W, W), W)

    def by_head(src, dst):
        wide = src[...].astype(F32).reshape(T, 2, KVH * D).transpose(1, 0, 2).astype(BF)
        for h in range(KVH):
            for kv in (0, 1):
                dst[h, kv] = wide[kv, :, h * D:(h + 1) * D]

    by_head(prompt, pkv)
    live[...] = (lax.broadcasted_iota(jnp.int32, (16, T), 1) < lengths[0]).astype(F32).astype(BF)
    pl.semaphore_wait(barrier, len(peers))

    def direct(a, kv, p, core):
        head = (mine if core == 0 else other) + a
        return remote(pkv.at[head, kv], kvb.at[a, kv, BACK[p], rows, :],
                      d_s.at[a, kv, BACK[p], core], d_r.at[a, kv, BACK[p], core], device(p, core))

    near = (3, 1, 2)

    def direct_start(a, kv):
        for p in near:
            direct(a, kv, p, 0).start()
            direct(a, kv, p, 1).start()

    def exchange(k, src_other, src_mine, dst_other, dst_mine):
        away = remote(src_other, dst_other, st_s.at[k], st_r.at[k], sib)
        away.start()
        here = pltpu.make_async_copy(src_mine, dst_mine, loc.at[k])
        here.start()
        return away, here

    def exchange_wait(pair):
        pair[0].wait_recv()
        pair[1].wait()

    def heads_of(which):
        return pl.ds(which, 2)

    direct_start(0, 0)
    ex_q = exchange(0, query.at[:, columns(1 - c)], query.at[:, columns(c)], xq.at[1], xq.at[0])
    ex_kv = exchange(1, pkv.at[heads_of(other)], pkv.at[heads_of(mine)],
                     kvb.at[:, :, 0, rows, :], kvb.at[:, :, 0, rows, :])
    direct_start(0, 1)
    direct_start(1, 0)
    direct_start(1, 1)
    by_head(resp, rkv)
    ex_r = exchange(2, rkv.at[heads_of(other)], rkv.at[heads_of(mine)], xr.at[:, 1], xr.at[:, 0])
    ex_g = exchange(3, grad.at[:, columns(1 - c)], grad.at[:, columns(c)], xg.at[1], xg.at[0])
    ex_l = exchange(4, live, live, xl.at[1], xl.at[0])

    def ag(a, kv, kind):
        to = {3: 2, 4: 1, 5: 2, 6: 1, 7: 3}[kind]
        src = {3: 3, 4: 3, 5: 1, 6: 2, 7: 6}[kind]
        dst = {3: 4, 4: 5, 5: 6, 6: 6, 7: 7}[kind]
        part = {5: pl.ds(0, T), 6: pl.ds(T, T)}.get(kind, pl.ds(0, BLK))
        return remote(kvb.at[a, kv, src, part, :], kvb.at[a, kv, dst, part, :],
                      ag_s.at[a, kv, kind - 3], ag_r.at[a, kv, kind - 3], device(to, 0))

    def ag_second(a, kv):
        for p in near:
            direct(a, kv, BACK[p], 0).wait_recv()
            direct(a, kv, BACK[p], 1).wait_recv()
        for k in (5, 6, 3, 4):
            ag(a, kv, k).start()

    def ag_third(a, kv):
        ag(a, kv, 5).wait_recv()
        ag(a, kv, 6).wait_recv()
        ag(a, kv, 7).start()

    def ag_wait(a, kv, *kinds):
        for k in kinds:
            ag(a, kv, k).wait_recv()

    def rs(a, kind):
        to = {3: 1, 4: 2, 5: 1, 6: 2}[kind]
        src = {3: 4, 4: 5, 5: 6, 6: 6}[kind]
        part = {5: pl.ds(0, T), 6: pl.ds(T, T)}.get(kind, pl.ds(0, BLK))
        return remote(pb.at[a, :, src, part, :], rb.at[a, kind - 3, :, part, :],
                      rs_s.at[a, kind - 3], rs_r.at[a, kind - 3], device(to, 0))

    def rs_last(a, p, core):
        slot = LAST[BACK[p]]
        return remote(pb.at[a, :, p, rows if core == 0 else orows, :], rbf.at[a, slot, core],
                      fin_s.at[a, slot, core], fin_r.at[a, slot, core], device(p, core))

    def last_start(a, p):
        rs_last(a, p, 0).start()
        rs_last(a, p, 1).start()

    def sum_three(a):
        rs(a, 3).wait_recv()
        rs(a, 4).wait_recv()
        pb[a, :, 3] = (pb[a, :, 3].astype(F32) + rb[a, 0].astype(F32) + rb[a, 1].astype(F32)).astype(BF)
        last_start(a, 3)

    def sum_two(a):
        rs(a, 6).wait_recv()
        pb[a, :, 2, T:] = (pb[a, :, 2, T:].astype(F32) + rb[a, 3, :, T:].astype(F32)).astype(BF)
        last_start(a, 2)

    def sum_one(a):
        rs(a, 5).wait_recv()
        pb[a, :, 1, :T] = (pb[a, :, 1, :T].astype(F32) + rb[a, 2, :, :T].astype(F32)).astype(BF)
        last_start(a, 1)

    def rs_final(a):
        rs_last(a, 0, 1).wait_recv()
        for p in (1, 2, 3, 7):
            for core in (0, 1):
                rs_last(a, BACK[p], core).wait_recv()
        for core in (0, 1):
            total = pb[a, :, 0, rows, :] if core == 0 else rbf[a, 0, 1]
            total = total.astype(F32)
            for slot in (1, 2, 3, 4):
                total = total + rbf[a, slot, core].astype(F32)
            rf[(mine if core == 0 else other) + a, 1] = total.astype(BF)
        for h in (a, 2 + a):
            for kv in (0, 1):
                pout[:, kv, h * D:(h + 1) * D] = rf[h, 1, kv]

    def place(a):
        return pl.ds(pl.multiple_of((2 * c + a) * (G * D), G * D), G * D)

    def o_copy(a):
        return remote(osend.at[a], oout.at[:, place(a)], out_s.at[a, 0], out_r.at[a, 0], sib)

    def q_copy(a):
        return remote(qsend.at[a], qout.at[:, place(a)], out_s.at[a, 1], out_r.at[a, 1], sib)

    def r_copy(a):
        return remote(rsend.at[a], rf.at[2 * c + a, 0], out_s.at[a, 2], out_r.at[a, 2], sib)

    def at_step(i, hooks):
        for k, calls in hooks.items():
            @pl.when(i == k)
            def _():
                for call in calls:
                    call()

    def stacked(ref, a, b):
        return jnp.concatenate([ref[b, :, (a * G + g) * D:(a * G + g + 1) * D] for g in range(G)], axis=0)

    def queries_of(a):
        return jnp.concatenate([stacked(xq, a, 0), stacked(xq, a, 1)], axis=0)

    def fold(value, op):
        n = value.shape[0]
        return op(value.reshape(n // 8, 8, R), axis=0)

    def shard(a, kv, j):
        return kvb[a, kv, pl.ds(j * STEP, STEP)].reshape(N, D)

    def scores(a, half, hooks):
        def step(i, _):
            at_step(i, hooks)
            s = dot(shard(a, 0, half * HALF + i), queries_of(a), 1, 1)
            sb[i] = s
            mb[...] = jnp.maximum(mb[...], fold(s, jnp.max))
            return 0

        lax.fori_loop(0, HALF, step, 0)

    def weigh(a, half, hooks):
        def step(i, _):
            at_step(i, hooks)
            j = half * HALF + i
            e = jnp.exp2(sb[i] * SCALE2 - tp[a] * SCALE2)
            lb[a] += fold(e, jnp.sum)
            low = e.astype(BF)
            eb[a, j] = low
            ot[a] += dot(shard(a, 1, j), low, 0, 0)
            return 0

        lax.fori_loop(0, HALF, step, 0)

    def first_half(a, hooks_a, hooks_b, before_values):
        slot = lax.broadcasted_iota(jnp.int32, (T, G, T), 2).reshape(T, COLS)
        key = lax.broadcasted_iota(jnp.int32, (T, COLS), 0)
        for b in (0, 1):
            s = dot(xr[a, b, 0], stacked(xq, a, b), 1, 1)
            srb[:, b * COLS:(b + 1) * COLS] = jnp.where(key <= slot, s, MASKED)
        mb[...] = fold(srb[...], jnp.max)
        scores(a, 0, hooks_a)
        tp[a] = jnp.max(mb[...], axis=0, keepdims=True)
        er = jnp.exp2(srb[...] * SCALE2 - tp[a] * SCALE2)
        lb[a] = fold(er, jnp.sum)
        erb[a] = er.astype(BF)
        for b in (0, 1):
            cols = slice(b * COLS, (b + 1) * COLS)
            ot[a, :, cols] = dot(xr[a, b, 1], erb[a, :, cols], 0, 0)
        before_values()
        weigh(a, 0, hooks_b)

    def second_half(a, hooks_a, hooks_b):
        mb[...] = jnp.broadcast_to(tp[a], (8, R))
        scores(a, 1, hooks_a)
        top = jnp.max(mb[...], axis=0, keepdims=True)
        shrink = jnp.exp2((tp[a] - top) * SCALE2)
        tp[a] = top
        fr[a] = shrink
        lb[a] = lb[a] * shrink
        ot[a] = ot[a] * shrink
        weigh(a, 1, hooks_b)

    def rowwise(a):
        inv = 1.0 / jnp.sum(lb[a], axis=0, keepdims=True)
        for b in (0, 1):
            on = xl[b, 0:1, :].astype(F32) > 0.0
            for g in range(G):
                lo = b * COLS + g * T
                cols = slice(lo, lo + T)
                hd = slice((a * G + g) * D, (a * G + g + 1) * D)
                att = ot[a, :, cols] * inv[:, cols]
                gt = jnp.where(on, xg[b, :, hd].astype(F32).T, 0.0)
                delta = jnp.sum(gt * att, axis=0, keepdims=True) * inv[:, cols]
                gt = gt * inv[:, cols]
                shrink = fr[a, :, cols]
                dlt[a, 0, :, cols] = delta * shrink
                dlt[a, 1, :, cols] = delta
                gp[a, 0, cols, :] = (gt * shrink).T.astype(BF)
                gp[a, 1, cols, :] = gt.T.astype(BF)
                att = jnp.where(on, att, 0.0).T.astype(BF)
                if b == 0:
                    oout[:, pl.ds(pl.multiple_of((2 * c + a) * (G * D) + g * D, D), D)] = att
                else:
                    osend[a, :, g * D:(g + 1) * D] = att
        o_copy(a).start()

    def backward(a, half, ends, start):
        def step(i, _):
            j = HALF + i if half else HALF - 1 - i
            ps = pl.ds(j * STEP, STEP)
            scaled = gp[a, half]
            dp = dot(shard(a, 1, j), scaled, 1, 1) - dlt[a, half]
            ds = (eb[a, j].astype(F32) * dp).astype(BF)
            pb[a, 1, ps] = dot(eb[a, j], scaled, 1, 0).astype(BF).reshape(STEP, BLK, D)
            pb[a, 0, ps] = (dot(ds, queries_of(a), 1, 0) * INV_ROOT).astype(BF).reshape(STEP, BLK, D)
            dqt[a] += dot(shard(a, 0, j), ds, 0, 0)
            at_step(i, ends)
            return 0

        if start:
            dqt[a] = jnp.zeros((D, R), F32)
        lax.fori_loop(0, HALF, step, 0)

    def backward_own(a):
        for b in (0, 1):
            cols = slice(b * COLS, (b + 1) * COLS)
            dp = dot(xr[a, b, 1], gp[a, 0, cols, :], 1, 1) - dlt[a, 0, :, cols]
            ds = (erb[a, :, cols].astype(F32) * dp).astype(BF)
            dv = dot(erb[a, :, cols], gp[a, 0, cols, :], 1, 0).astype(BF)
            dk = (dot(ds, stacked(xq, a, b), 1, 0) * INV_ROOT).astype(BF)
            dqt[a, :, cols] += dot(xr[a, b, 0], ds, 0, 0)
            if b == 0:
                rf[2 * c + a, 0, 0] = dk
                rf[2 * c + a, 0, 1] = dv
            else:
                rsend[a, 0] = dk
                rsend[a, 1] = dv
        r_copy(a).start()
        for b in (0, 1):
            for g in range(G):
                lo = b * COLS + g * T
                got = (dqt[a, :, lo:lo + T] * INV_ROOT).T.astype(BF)
                if b == 0:
                    qout[:, pl.ds(pl.multiple_of((2 * c + a) * (G * D) + g * D, D), D)] = got
                else:
                    qsend[a, :, g * D:(g + 1) * D] = got
        q_copy(a).start()

    f = functools.partial

    def far_ends(a):
        return {0: [rs(a, 3).start, rs(a, 4).start], 1: [rs(a, 5).start, rs(a, 6).start, f(last_start, a, 7)]}

    def near_ends(a):
        return {0: [f(sum_three, a), f(sum_two, a)], 1: [f(sum_one, a), rs_last(a, 0, 1).start]}

    for pair in (ex_q, ex_r, ex_kv):
        exchange_wait(pair)
    first_half(0, {0: [f(ag_second, 0, 0)]}, {}, f(ag_second, 0, 1))
    first_half(1, {0: [f(ag_second, 1, 0)]}, {0: [f(ag_third, 0, 0)]}, f(ag_second, 1, 1))
    second_half(0, {0: [f(ag_wait, 0, 0, 3, 4)], 1: [f(ag_third, 0, 1), f(ag_wait, 0, 0, 7)]},
                {0: [f(ag_third, 1, 0), f(ag_wait, 0, 1, 3, 4)], 1: [f(ag_third, 1, 1), f(ag_wait, 0, 1, 7)]})
    exchange_wait(ex_g)
    exchange_wait(ex_l)
    rowwise(0)
    backward(0, 1, far_ends(0), True)
    second_half(1, {0: [f(ag_wait, 1, 0, 3, 4)], 1: [f(ag_wait, 1, 0, 7)]},
                {0: [f(ag_wait, 1, 1, 3, 4)], 1: [f(ag_wait, 1, 1, 7)]})
    rowwise(1)
    backward(1, 1, far_ends(1), True)
    backward(0, 0, near_ends(0), False)
    backward(1, 0, near_ends(1), False)
    backward_own(0)
    backward_own(1)
    rs_final(0)
    r_copy(0).wait()
    r_copy(1).wait()
    for h in range(KVH):
        for kv in (0, 1):
            rout[:, kv, h * D:(h + 1) * D] = rf[h, 0, kv]
    rs_final(1)

    for away, _ in (ex_q, ex_kv, ex_r, ex_g, ex_l):
        away.wait_send()
    for a in (0, 1):
        for kv in (0, 1):
            for p in near:
                direct(a, kv, p, 0).wait_send()
                direct(a, kv, p, 1).wait_send()
            for kind in range(3, 8):
                ag(a, kv, kind).wait_send()
        for kind in range(3, 7):
            rs(a, kind).wait_send()
        rs_last(a, 0, 1).wait_send()
        for p in (1, 2, 3, 7):
            rs_last(a, p, 0).wait_send()
            rs_last(a, p, 1).wait_send()
        o_copy(a).wait()
        q_copy(a).wait()


def per_device(prompt_kv, queries, response_key_values, grad_out, lengths):
    vmem = pl.BlockSpec(memory_space=pltpu.VMEM)
    dma = pltpu.SemaphoreType.DMA
    flops = 6 * 2 * 2 * R * (NP * BLK + T) * D
    return pl.pallas_call(
        kernel,
        out_shape=(
            jax.ShapeDtypeStruct(queries.shape, BF),
            jax.ShapeDtypeStruct(queries.shape, BF),
            jax.ShapeDtypeStruct(prompt_kv.shape, BF),
            jax.ShapeDtypeStruct(prompt_kv.shape, BF),
        ),
        in_specs=[pl.BlockSpec(memory_space=pltpu.SMEM)] + [vmem] * 4,
        out_specs=(vmem,) * 4,
        scratch_shapes=[
            pltpu.VMEM((KVH, 2, T, D), BF),
            pltpu.VMEM((KVH, 2, T, D), BF),
            pltpu.VMEM((16, T), BF),
            pltpu.VMEM((2, 2, NP, BLK, D), BF),
            pltpu.VMEM((2, T, 2 * G * D), BF),
            pltpu.VMEM((2, T, 2 * G * D), BF),
            pltpu.VMEM((2, 2, 2, T, D), BF),
            pltpu.VMEM((2, 16, T), BF),
            pltpu.VMEM((HALF, N, R), F32),
            pltpu.VMEM((T, R), F32),
            pltpu.VMEM((2, NI, N, R), BF),
            pltpu.VMEM((2, T, R), BF),
            pltpu.VMEM((8, R), F32),
            pltpu.VMEM((2, 1, R), F32),
            pltpu.VMEM((2, 8, R), F32),
            pltpu.VMEM((2, D, R), F32),
            pltpu.VMEM((2, 1, R), F32),
            pltpu.VMEM((2, 2, R, D), BF),
            pltpu.VMEM((2, 2, 1, R), F32),
            pltpu.VMEM((2, D, R), F32),
            pltpu.VMEM((2, T, G * D), BF),
            pltpu.VMEM((2, T, G * D), BF),
            pltpu.VMEM((KVH, 2, 2, T, D), BF),
            pltpu.VMEM((2, 2, T, D), BF),
            pltpu.VMEM((2, 2, NP, BLK, D), BF),
            pltpu.VMEM((2, 4, 2, BLK, D), BF),
            pltpu.VMEM((2, 5, 2, 2, T, D), BF),
            dma((5,)), dma((5,)), dma((5,)),
            dma((2, 2, 4, 2)), dma((2, 2, 4, 2)),
            dma((2, 2, 5)), dma((2, 2, 5)),
            dma((2, 4)), dma((2, 4)),
            dma((2, 5, 2)), dma((2, 5, 2)),
            dma((2, 3)), dma((2, 3)),
        ],
        compiler_params=pltpu.CompilerParams(
            collective_id=0, has_side_effects=True, vmem_limit_bytes=56 << 20),
        cost_estimate=pl.CostEstimate(flops=flops, bytes_accessed=8 << 20, transcendentals=2 * R * (NP * BLK + T)),
        name="shared_prompt_attention",
    )(lengths, prompt_kv, response_key_values, queries, grad_out)


def solution(mesh):
    wide, thick = P(("grp", "resp"), None), P(("grp", "resp"), None, None)
    return jax.shard_map(
        per_device,
        mesh=mesh,
        in_specs=(thick, wide, thick, wide, P(("grp", "resp"))),
        out_specs=(wide, wide, thick, thick),
        check_vma=False,
    )
```

```python
import functools
import math

import jax
import jax.numpy as jnp
from jax import lax
from jax.experimental import pallas as pl
from jax.experimental.pallas import tpu as pltpu
from jax.sharding import PartitionSpec as P

D = 128
T = 128
G = 5
KVH = 4
BLK = 2 * T
COLS = G * T
R = 2 * COLS
NP = 8
MASKED = -1e30
INV_ROOT = 1.0 / math.sqrt(D)
SCALE2 = INV_ROOT * math.log2(math.e)
BF = jnp.bfloat16
F32 = jnp.float32
MESH = pl.DeviceIdType.MESH


def dot(a, b, ca, cb):
    return lax.dot_general(a, b, (((ca,), (cb,)), ((), ())), preferred_element_type=F32)


STEP = 2
NI = NP // STEP
N = STEP * BLK
HALF = NI // 2
BACK = (0, 2, 1, 3, 5, 4, 6, 7)
LAST = {0: 0, 1: 1, 2: 2, 3: 3, 7: 4}


def kernel(lengths, prompt, resp, query, grad, oout, qout, rout, pout,
           pkv, rkv, live, kvb, xq, xg, xr, xl, sb, srb, eb, erb, mb, tp, lb, ot, fr, gp, dlt, dqt,
           osend, qsend, rf, rsend, pb, rb, rbf,
           st_s, st_r, loc, d_s, d_r, ag_s, ag_r, rs_s, rs_r, fin_s, fin_r, out_s, out_r, own):
    me = lax.axis_index("resp")
    z, x, c = me // 8, (me // 2) % 4, me % 2

    def device(p, core):
        dx = (0, 3, 1, 0, 3, 1, 2, 2)[p]
        zz = z if p in (0, 1, 2, 6) else 1 - z
        cc = c if core == 0 else 1 - c
        return zz * 8 + ((x + dx) % 4) * 2 + cc

    def remote(src, dst, ss, rs, to):
        return pltpu.make_async_remote_copy(
            src_ref=src, dst_ref=dst, send_sem=ss, recv_sem=rs, device_id={"resp": to}, device_id_type=MESH)

    barrier = pltpu.get_barrier_semaphore()
    peers = [(p, core) for p in (0, 1, 2, 3, 7) for core in (0, 1) if p or core]
    for p, core in peers:
        pl.semaphore_signal(barrier, inc=1, device_id={"resp": device(p, core)}, device_id_type=MESH)

    sib = device(0, 1)
    mine, other = 2 * c, 2 * (1 - c)
    rows = pl.ds(pl.multiple_of(c * T, T), T)
    orows = pl.ds(pl.multiple_of((1 - c) * T, T), T)
    W = 2 * G * D

    def columns(which):
        return pl.ds(pl.multiple_of(which * W, W), W)

    def by_head(src, dst):
        wide = src[...].astype(F32).reshape(T, 2, KVH * D).transpose(1, 0, 2).astype(BF)
        for h in range(KVH):
            for kv in (0, 1):
                dst[h, kv] = wide[kv, :, h * D:(h + 1) * D]

    by_head(prompt, pkv)
    live[...] = (lax.broadcasted_iota(jnp.int32, (16, T), 1) < lengths[0]).astype(F32).astype(BF)
    pl.semaphore_wait(barrier, len(peers))

    def direct(a, kv, p, core):
        head = (mine if core == 0 else other) + a
        return remote(pkv.at[head, kv], kvb.at[a, kv, BACK[p], rows, :],
                      d_s.at[a, kv, BACK[p], core], d_r.at[a, kv, BACK[p], core], device(p, core))

    near = (3, 1, 2)

    def direct_start(a, kv):
        for p in near:
            direct(a, kv, p, 0).start()
            direct(a, kv, p, 1).start()

    def exchange(k, src_other, src_mine, dst_other, dst_mine):
        away = remote(src_other, dst_other, st_s.at[k], st_r.at[k], sib)
        away.start()
        here = pltpu.make_async_copy(src_mine, dst_mine, loc.at[k])
        here.start()
        return away, here

    def exchange_wait(pair):
        pair[0].wait_recv()
        pair[1].wait()

    def heads_of(which):
        return pl.ds(which, 2)

    direct_start(0, 0)
    ex_q = exchange(0, query.at[:, columns(1 - c)], query.at[:, columns(c)], xq.at[1], xq.at[0])
    ex_kv = exchange(1, pkv.at[heads_of(other)], pkv.at[heads_of(mine)],
                     kvb.at[:, :, 0, rows, :], kvb.at[:, :, 0, rows, :])
    direct_start(0, 1)
    direct_start(1, 0)
    direct_start(1, 1)
    by_head(resp, rkv)
    ex_r = exchange(2, rkv.at[heads_of(other)], rkv.at[heads_of(mine)], xr.at[:, 1], xr.at[:, 0])
    ex_g = exchange(3, grad.at[:, columns(1 - c)], grad.at[:, columns(c)], xg.at[1], xg.at[0])
    ex_l = exchange(4, live, live, xl.at[1], xl.at[0])

    def ag(a, kv, kind):
        to = {3: 2, 4: 1, 5: 2, 6: 1, 7: 3}[kind]
        src = {3: 3, 4: 3, 5: 1, 6: 2, 7: 6}[kind]
        dst = {3: 4, 4: 5, 5: 6, 6: 6, 7: 7}[kind]
        part = {5: pl.ds(0, T), 6: pl.ds(T, T)}.get(kind, pl.ds(0, BLK))
        return remote(kvb.at[a, kv, src, part, :], kvb.at[a, kv, dst, part, :],
                      ag_s.at[a, kv, kind - 3], ag_r.at[a, kv, kind - 3], device(to, 0))

    def ag_second(a, kv):
        for p in near:
            direct(a, kv, BACK[p], 0).wait_recv()
            direct(a, kv, BACK[p], 1).wait_recv()
        for k in (5, 6, 3, 4):
            ag(a, kv, k).start()

    def ag_third(a, kv):
        ag(a, kv, 5).wait_recv()
        ag(a, kv, 6).wait_recv()
        ag(a, kv, 7).start()

    def ag_wait(a, kv, *kinds):
        for k in kinds:
            ag(a, kv, k).wait_recv()

    def rs(a, kind):
        to = {3: 1, 4: 2, 5: 1, 6: 2}[kind]
        src = {3: 4, 4: 5, 5: 6, 6: 6}[kind]
        part = {5: pl.ds(0, T), 6: pl.ds(T, T)}.get(kind, pl.ds(0, BLK))
        return remote(pb.at[a, :, src, part, :], rb.at[a, kind - 3, :, part, :],
                      rs_s.at[a, kind - 3], rs_r.at[a, kind - 3], device(to, 0))

    def rs_last(a, p, core):
        slot = LAST[BACK[p]]
        return remote(pb.at[a, :, p, rows if core == 0 else orows, :], rbf.at[a, slot, core],
                      fin_s.at[a, slot, core], fin_r.at[a, slot, core], device(p, core))

    def last_start(a, p):
        rs_last(a, p, 0).start()
        rs_last(a, p, 1).start()

    def sum_three(a):
        rs(a, 3).wait_recv()
        rs(a, 4).wait_recv()
        pb[a, :, 3] = (pb[a, :, 3].astype(F32) + rb[a, 0].astype(F32) + rb[a, 1].astype(F32)).astype(BF)
        last_start(a, 3)

    def sum_two(a):
        rs(a, 6).wait_recv()
        pb[a, :, 2, T:] = (pb[a, :, 2, T:].astype(F32) + rb[a, 3, :, T:].astype(F32)).astype(BF)
        last_start(a, 2)

    def sum_one(a):
        rs(a, 5).wait_recv()
        pb[a, :, 1, :T] = (pb[a, :, 1, :T].astype(F32) + rb[a, 2, :, :T].astype(F32)).astype(BF)
        last_start(a, 1)

    def rs_final(a):
        rs_last(a, 0, 1).wait_recv()
        for p in (1, 2, 3, 7):
            for core in (0, 1):
                rs_last(a, BACK[p], core).wait_recv()
        for core in (0, 1):
            total = pb[a, :, 0, rows, :] if core == 0 else rbf[a, 0, 1]
            total = total.astype(F32)
            for slot in (1, 2, 3, 4):
                total = total + rbf[a, slot, core].astype(F32)
            rf[(mine if core == 0 else other) + a, 1] = total.astype(BF)
        for h in (a, 2 + a):
            for kv in (0, 1):
                pout[:, kv, h * D:(h + 1) * D] = rf[h, 1, kv]

    def place(a):
        return pl.ds(pl.multiple_of((2 * c + a) * (G * D), G * D), G * D)

    def o_copy(a):
        return remote(osend.at[a, 1], oout.at[:, place(a)], out_s.at[a, 0], out_r.at[a, 0], sib)

    def q_copy(a):
        return remote(qsend.at[a, 1], qout.at[:, place(a)], out_s.at[a, 1], out_r.at[a, 1], sib)

    def o_own(a):
        return pltpu.make_async_copy(osend.at[a, 0], oout.at[:, place(a)], own.at[a, 0])

    def q_own(a):
        return pltpu.make_async_copy(qsend.at[a, 0], qout.at[:, place(a)], own.at[a, 1])

    def r_copy(a):
        return remote(rsend.at[a], rf.at[2 * c + a, 0], out_s.at[a, 2], out_r.at[a, 2], sib)

    def at_step(i, hooks):
        for k, calls in hooks.items():
            @pl.when(i == k)
            def _():
                for call in calls:
                    call()

    def stacked(ref, a, b):
        return jnp.concatenate([ref[b, :, (a * G + g) * D:(a * G + g + 1) * D] for g in range(G)], axis=0)

    def queries_of(a):
        return jnp.concatenate([stacked(xq, a, 0), stacked(xq, a, 1)], axis=0)

    def fold(value, op):
        n = value.shape[0]
        return op(value.reshape(n // 8, 8, R), axis=0)

    def shard(a, kv, j):
        return kvb[a, kv, pl.ds(j * STEP, STEP)].reshape(N, D)

    def scores(a, half, hooks):
        def step(i, _):
            at_step(i, hooks)
            s = dot(shard(a, 0, half * HALF + i), queries_of(a), 1, 1)
            sb[i] = s
            mb[...] = jnp.maximum(mb[...], fold(s, jnp.max))
            return 0

        lax.fori_loop(0, HALF, step, 0)

    def weigh(a, half, hooks):
        def step(i, _):
            at_step(i, hooks)
            j = half * HALF + i
            e = jnp.exp2(sb[i] * SCALE2 - tp[a] * SCALE2)
            lb[a] += fold(e, jnp.sum)
            low = e.astype(BF)
            eb[a, j] = low
            ot[a] += dot(shard(a, 1, j), low, 0, 0)
            return 0

        lax.fori_loop(0, HALF, step, 0)

    def first_half(a, hooks_a, hooks_b, before_values):
        slot = lax.broadcasted_iota(jnp.int32, (T, G, T), 2).reshape(T, COLS)
        key = lax.broadcasted_iota(jnp.int32, (T, COLS), 0)
        for b in (0, 1):
            s = dot(xr[a, b, 0], stacked(xq, a, b), 1, 1)
            srb[:, b * COLS:(b + 1) * COLS] = jnp.where(key <= slot, s, MASKED)
        mb[...] = fold(srb[...], jnp.max)
        scores(a, 0, hooks_a)
        tp[a] = jnp.max(mb[...], axis=0, keepdims=True)
        er = jnp.exp2(srb[...] * SCALE2 - tp[a] * SCALE2)
        lb[a] = fold(er, jnp.sum)
        erb[a] = er.astype(BF)
        for b in (0, 1):
            cols = slice(b * COLS, (b + 1) * COLS)
            ot[a, :, cols] = dot(xr[a, b, 1], erb[a, :, cols], 0, 0)
        before_values()
        weigh(a, 0, hooks_b)

    def second_half(a, hooks_a, hooks_b):
        mb[...] = jnp.broadcast_to(tp[a], (8, R))
        scores(a, 1, hooks_a)
        top = jnp.max(mb[...], axis=0, keepdims=True)
        shrink = jnp.exp2((tp[a] - top) * SCALE2)
        tp[a] = top
        fr[a] = shrink
        lb[a] = lb[a] * shrink
        ot[a] = ot[a] * shrink
        weigh(a, 1, hooks_b)

    def rowwise(a):
        inv = 1.0 / jnp.sum(lb[a], axis=0, keepdims=True)
        for b in (0, 1):
            on = xl[b, 0:1, :].astype(F32) > 0.0
            for g in range(G):
                lo = b * COLS + g * T
                cols = slice(lo, lo + T)
                hd = slice((a * G + g) * D, (a * G + g + 1) * D)
                att = ot[a, :, cols] * inv[:, cols]
                gt = jnp.where(on, xg[b, :, hd].astype(F32).T, 0.0)
                delta = jnp.sum(gt * att, axis=0, keepdims=True) * inv[:, cols]
                gt = gt * inv[:, cols]
                shrink = fr[a, :, cols]
                dlt[a, 0, :, cols] = delta * shrink
                dlt[a, 1, :, cols] = delta
                gp[a, 0, cols, :] = (gt * shrink).T.astype(BF)
                gp[a, 1, cols, :] = gt.T.astype(BF)
                att = jnp.where(on, att, 0.0).T.astype(BF)
                osend[a, b, :, g * D:(g + 1) * D] = att
        o_copy(a).start()
        o_own(a).start()

    def backward(a, half, ends, start):
        def step(i, _):
            j = HALF + i if half else HALF - 1 - i
            ps = pl.ds(j * STEP, STEP)
            scaled = gp[a, half]
            dp = dot(shard(a, 1, j), scaled, 1, 1) - dlt[a, half]
            ds = (eb[a, j].astype(F32) * dp).astype(BF)
            pb[a, 1, ps] = dot(eb[a, j], scaled, 1, 0).astype(BF).reshape(STEP, BLK, D)
            pb[a, 0, ps] = (dot(ds, queries_of(a), 1, 0) * INV_ROOT).astype(BF).reshape(STEP, BLK, D)
            dqt[a] += dot(shard(a, 0, j), ds, 0, 0)
            at_step(i, ends)
            return 0

        if start:
            dqt[a] = jnp.zeros((D, R), F32)
        lax.fori_loop(0, HALF, step, 0)

    def backward_own(a):
        for b in (0, 1):
            cols = slice(b * COLS, (b + 1) * COLS)
            dp = dot(xr[a, b, 1], gp[a, 0, cols, :], 1, 1) - dlt[a, 0, :, cols]
            ds = (erb[a, :, cols].astype(F32) * dp).astype(BF)
            dv = dot(erb[a, :, cols], gp[a, 0, cols, :], 1, 0).astype(BF)
            dk = (dot(ds, stacked(xq, a, b), 1, 0) * INV_ROOT).astype(BF)
            dqt[a, :, cols] += dot(xr[a, b, 0], ds, 0, 0)
            if b == 0:
                rf[2 * c + a, 0, 0] = dk
                rf[2 * c + a, 0, 1] = dv
            else:
                rsend[a, 0] = dk
                rsend[a, 1] = dv
        r_copy(a).start()
        for b in (0, 1):
            for g in range(G):
                lo = b * COLS + g * T
                got = (dqt[a, :, lo:lo + T] * INV_ROOT).T.astype(BF)
                qsend[a, b, :, g * D:(g + 1) * D] = got
        q_copy(a).start()
        q_own(a).start()

    f = functools.partial

    def far_ends(a):
        return {0: [rs(a, 3).start, rs(a, 4).start], 1: [rs(a, 5).start, rs(a, 6).start, f(last_start, a, 7)]}

    def near_ends(a):
        return {0: [f(sum_three, a), f(sum_two, a)], 1: [f(sum_one, a), rs_last(a, 0, 1).start]}

    for pair in (ex_q, ex_r, ex_kv):
        exchange_wait(pair)
    first_half(0, {0: [f(ag_second, 0, 0)]}, {}, f(ag_second, 0, 1))
    first_half(1, {0: [f(ag_second, 1, 0)]}, {0: [f(ag_third, 0, 0)]}, f(ag_second, 1, 1))
    second_half(0, {0: [f(ag_wait, 0, 0, 3, 4)], 1: [f(ag_third, 0, 1), f(ag_wait, 0, 0, 7)]},
                {0: [f(ag_third, 1, 0), f(ag_wait, 0, 1, 3, 4)], 1: [f(ag_third, 1, 1), f(ag_wait, 0, 1, 7)]})
    exchange_wait(ex_g)
    exchange_wait(ex_l)
    rowwise(0)
    backward(0, 1, far_ends(0), True)
    second_half(1, {0: [f(ag_wait, 1, 0, 3, 4)], 1: [f(ag_wait, 1, 0, 7)]},
                {0: [f(ag_wait, 1, 1, 3, 4)], 1: [f(ag_wait, 1, 1, 7)]})
    rowwise(1)
    backward(1, 1, far_ends(1), True)
    backward(0, 0, near_ends(0), False)
    backward(1, 0, near_ends(1), False)
    backward_own(0)
    backward_own(1)
    rs_final(0)
    r_copy(0).wait()
    r_copy(1).wait()
    for h in range(KVH):
        for kv in (0, 1):
            rout[:, kv, h * D:(h + 1) * D] = rf[h, 0, kv]
    rs_final(1)

    for away, _ in (ex_q, ex_kv, ex_r, ex_g, ex_l):
        away.wait_send()
    for a in (0, 1):
        for kv in (0, 1):
            for p in near:
                direct(a, kv, p, 0).wait_send()
                direct(a, kv, p, 1).wait_send()
            for kind in range(3, 8):
                ag(a, kv, kind).wait_send()
        for kind in range(3, 7):
            rs(a, kind).wait_send()
        rs_last(a, 0, 1).wait_send()
        for p in (1, 2, 3, 7):
            rs_last(a, p, 0).wait_send()
            rs_last(a, p, 1).wait_send()
        o_copy(a).wait()
        q_copy(a).wait()
        o_own(a).wait()
        q_own(a).wait()


def hand_over(*refs):
    sources, targets, staged, sems = refs[:4], refs[4:8], refs[8:12], refs[12]
    arrive = [pltpu.make_async_copy(sources[k], staged[k], sems.at[0, k]) for k in range(4)]
    leave = [pltpu.make_async_copy(staged[k], targets[k], sems.at[1, k]) for k in range(4)]
    for copy in arrive:
        copy.start()
    for k in range(4):
        arrive[k].wait()
        leave[k].start()
    for copy in leave:
        copy.wait()


def per_device(prompt_kv, queries, response_key_values, grad_out, lengths):
    vmem = pl.BlockSpec(memory_space=pltpu.VMEM)
    anywhere = pl.BlockSpec(memory_space=pl.ANY)
    dma = pltpu.SemaphoreType.DMA
    flops = 6 * 2 * 2 * R * (NP * BLK + T) * D
    found = pl.pallas_call(
        kernel,
        out_shape=(
            jax.ShapeDtypeStruct(queries.shape, BF),
            jax.ShapeDtypeStruct(queries.shape, BF),
            jax.ShapeDtypeStruct(prompt_kv.shape, BF),
            jax.ShapeDtypeStruct(prompt_kv.shape, BF),
        ),
        in_specs=[pl.BlockSpec(memory_space=pltpu.SMEM), vmem, vmem, anywhere, anywhere],
        out_specs=(anywhere, anywhere, vmem, vmem),
        scratch_shapes=[
            pltpu.VMEM((KVH, 2, T, D), BF),
            pltpu.VMEM((KVH, 2, T, D), BF),
            pltpu.VMEM((16, T), BF),
            pltpu.VMEM((2, 2, NP, BLK, D), BF),
            pltpu.VMEM((2, T, 2 * G * D), BF),
            pltpu.VMEM((2, T, 2 * G * D), BF),
            pltpu.VMEM((2, 2, 2, T, D), BF),
            pltpu.VMEM((2, 16, T), BF),
            pltpu.VMEM((HALF, N, R), F32),
            pltpu.VMEM((T, R), F32),
            pltpu.VMEM((2, NI, N, R), BF),
            pltpu.VMEM((2, T, R), BF),
            pltpu.VMEM((8, R), F32),
            pltpu.VMEM((2, 1, R), F32),
            pltpu.VMEM((2, 8, R), F32),
            pltpu.VMEM((2, D, R), F32),
            pltpu.VMEM((2, 1, R), F32),
            pltpu.VMEM((2, 2, R, D), BF),
            pltpu.VMEM((2, 2, 1, R), F32),
            pltpu.VMEM((2, D, R), F32),
            pltpu.VMEM((2, 2, T, G * D), BF),
            pltpu.VMEM((2, 2, T, G * D), BF),
            pltpu.VMEM((KVH, 2, 2, T, D), BF),
            pltpu.VMEM((2, 2, T, D), BF),
            pltpu.VMEM((2, 2, NP, BLK, D), BF),
            pltpu.VMEM((2, 4, 2, BLK, D), BF),
            pltpu.VMEM((2, 5, 2, 2, T, D), BF),
            dma((5,)), dma((5,)), dma((5,)),
            dma((2, 2, 4, 2)), dma((2, 2, 4, 2)),
            dma((2, 2, 5)), dma((2, 2, 5)),
            dma((2, 4)), dma((2, 4)),
            dma((2, 5, 2)), dma((2, 5, 2)),
            dma((2, 3)), dma((2, 3)), dma((2, 2)),
        ],
        compiler_params=pltpu.CompilerParams(
            collective_id=0, has_side_effects=True, vmem_limit_bytes=56 << 20),
        cost_estimate=pl.CostEstimate(flops=flops, bytes_accessed=8 << 20, transcendentals=2 * R * (NP * BLK + T)),
        name="shared_prompt_attention",
    )(lengths, prompt_kv, response_key_values, queries, grad_out)
    return pl.pallas_call(
        hand_over,
        out_shape=tuple(jax.ShapeDtypeStruct(v.shape, v.dtype) for v in found),
        in_specs=[anywhere] * 4,
        out_specs=(anywhere,) * 4,
        scratch_shapes=[pltpu.VMEM(v.shape, v.dtype) for v in found] + [dma((2, 4))],
        name="hand_over",
    )(*found)


def solution(mesh):
    wide, thick = P(("grp", "resp"), None), P(("grp", "resp"), None, None)
    return jax.shard_map(
        per_device,
        mesh=mesh,
        in_specs=(thick, wide, thick, wide, P(("grp", "resp"))),
        out_specs=(wide, wide, thick, thick),
        check_vma=False,
    )
```

```python
import functools
import math

import jax
import jax.numpy as jnp
from jax import lax
from jax.experimental import pallas as pl
from jax.experimental.pallas import tpu as pltpu
from jax.sharding import PartitionSpec as P

D = 128
T = 128
G = 5
KVH = 4
BLK = 2 * T
COLS = G * T
R = 2 * COLS
NP = 8
MASKED = -1e30
INV_ROOT = 1.0 / math.sqrt(D)
SCALE2 = INV_ROOT * math.log2(math.e)
BF = jnp.bfloat16
F32 = jnp.float32
MESH = pl.DeviceIdType.MESH


def dot(a, b, ca, cb):
    return lax.dot_general(a, b, (((ca,), (cb,)), ((), ())), preferred_element_type=F32)


STEP = 2
NI = NP // STEP
N = STEP * BLK
HALF = NI // 2
BACK = (0, 2, 1, 3, 5, 4, 6, 7)
LAST = {0: 0, 1: 1, 2: 2, 3: 3, 7: 4}


def kernel(lengths, prompt, resp, query, grad, oout, qout, rout, pout,
           pkv, rkv, live, kvb, xq, xg, xr, xl, sb, srb, eb, erb, mb, tp, lb, ot, fr, gp, dlt, dqt,
           osend, qsend, rf, rsend, pb, rb, rbf,
           st_s, st_r, loc, d_s, d_r, ag_s, ag_r, rs_s, rs_r, fin_s, fin_r, out_s, out_r, own):
    me = lax.axis_index("resp")
    z, x, c = me // 8, (me // 2) % 4, me % 2

    def device(p, core):
        dx = (0, 3, 1, 0, 3, 1, 2, 2)[p]
        zz = z if p in (0, 1, 2, 6) else 1 - z
        cc = c if core == 0 else 1 - c
        return zz * 8 + ((x + dx) % 4) * 2 + cc

    def remote(src, dst, ss, rs, to):
        return pltpu.make_async_remote_copy(
            src_ref=src, dst_ref=dst, send_sem=ss, recv_sem=rs, device_id={"resp": to}, device_id_type=MESH)

    barrier = pltpu.get_barrier_semaphore()
    peers = [(p, core) for p in (0, 1, 2, 3, 7) for core in (0, 1) if p or core]
    for p, core in peers:
        pl.semaphore_signal(barrier, inc=1, device_id={"resp": device(p, core)}, device_id_type=MESH)

    sib = device(0, 1)
    mine, other = 2 * c, 2 * (1 - c)
    rows = pl.ds(pl.multiple_of(c * T, T), T)
    orows = pl.ds(pl.multiple_of((1 - c) * T, T), T)
    W = 2 * G * D

    def columns(which):
        return pl.ds(pl.multiple_of(which * W, W), W)

    def by_head(src, dst):
        wide = src[...].astype(F32).reshape(T, 2, KVH * D).transpose(1, 0, 2).astype(BF)
        for h in range(KVH):
            for kv in (0, 1):
                dst[h, kv] = wide[kv, :, h * D:(h + 1) * D]

    by_head(prompt, pkv)
    live[...] = (lax.broadcasted_iota(jnp.int32, (16, T), 1) < lengths[0]).astype(F32).astype(BF)
    pl.semaphore_wait(barrier, len(peers))

    def direct(a, kv, p, core):
        head = (mine if core == 0 else other) + a
        return remote(pkv.at[head, kv], kvb.at[a, kv, BACK[p], rows, :],
                      d_s.at[a, kv, BACK[p], core], d_r.at[a, kv, BACK[p], core], device(p, core))

    near = (3, 1, 2)

    def direct_start(a, kv):
        for p in near:
            direct(a, kv, p, 0).start()
            direct(a, kv, p, 1).start()

    def exchange(k, src_other, src_mine, dst_other, dst_mine):
        away = remote(src_other, dst_other, st_s.at[k], st_r.at[k], sib)
        away.start()
        here = pltpu.make_async_copy(src_mine, dst_mine, loc.at[k])
        here.start()
        return away, here

    def exchange_wait(pair):
        pair[0].wait_recv()
        pair[1].wait()

    def heads_of(which):
        return pl.ds(which, 2)

    direct_start(0, 0)
    ex_q = exchange(0, query.at[:, columns(1 - c)], query.at[:, columns(c)], xq.at[1], xq.at[0])
    ex_kv = exchange(1, pkv.at[heads_of(other)], pkv.at[heads_of(mine)],
                     kvb.at[:, :, 0, rows, :], kvb.at[:, :, 0, rows, :])
    direct_start(0, 1)
    direct_start(1, 0)
    direct_start(1, 1)
    by_head(resp, rkv)
    ex_r = exchange(2, rkv.at[heads_of(other)], rkv.at[heads_of(mine)], xr.at[:, 1], xr.at[:, 0])
    ex_g = exchange(3, grad.at[:, columns(1 - c)], grad.at[:, columns(c)], xg.at[1], xg.at[0])
    ex_l = exchange(4, live, live, xl.at[1], xl.at[0])

    def ag(a, kv, kind):
        to = {3: 2, 4: 1, 5: 2, 6: 1, 7: 3}[kind]
        src = {3: 3, 4: 3, 5: 1, 6: 2, 7: 6}[kind]
        dst = {3: 4, 4: 5, 5: 6, 6: 6, 7: 7}[kind]
        part = {5: pl.ds(0, T), 6: pl.ds(T, T)}.get(kind, pl.ds(0, BLK))
        return remote(kvb.at[a, kv, src, part, :], kvb.at[a, kv, dst, part, :],
                      ag_s.at[a, kv, kind - 3], ag_r.at[a, kv, kind - 3], device(to, 0))

    def ag_second(a, kv):
        for p in near:
            direct(a, kv, BACK[p], 0).wait_recv()
            direct(a, kv, BACK[p], 1).wait_recv()
        for k in (5, 6, 3, 4):
            ag(a, kv, k).start()

    def ag_third(a, kv):
        ag(a, kv, 5).wait_recv()
        ag(a, kv, 6).wait_recv()
        ag(a, kv, 7).start()

    def ag_wait(a, kv, *kinds):
        for k in kinds:
            ag(a, kv, k).wait_recv()

    def rs(a, kind):
        to = {3: 1, 4: 2, 5: 1, 6: 2}[kind]
        src = {3: 4, 4: 5, 5: 6, 6: 6}[kind]
        part = {5: pl.ds(0, T), 6: pl.ds(T, T)}.get(kind, pl.ds(0, BLK))
        return remote(pb.at[a, :, src, part, :], rb.at[a, kind - 3, :, part, :],
                      rs_s.at[a, kind - 3], rs_r.at[a, kind - 3], device(to, 0))

    def rs_last(a, p, core):
        slot = LAST[BACK[p]]
        return remote(pb.at[a, :, p, rows if core == 0 else orows, :], rbf.at[a, slot, core],
                      fin_s.at[a, slot, core], fin_r.at[a, slot, core], device(p, core))

    def last_start(a, p):
        rs_last(a, p, 0).start()
        rs_last(a, p, 1).start()

    def sum_three(a):
        rs(a, 3).wait_recv()
        rs(a, 4).wait_recv()
        pb[a, :, 3] = (pb[a, :, 3].astype(F32) + rb[a, 0].astype(F32) + rb[a, 1].astype(F32)).astype(BF)
        last_start(a, 3)

    def sum_two(a):
        rs(a, 6).wait_recv()
        pb[a, :, 2, T:] = (pb[a, :, 2, T:].astype(F32) + rb[a, 3, :, T:].astype(F32)).astype(BF)
        last_start(a, 2)

    def sum_one(a):
        rs(a, 5).wait_recv()
        pb[a, :, 1, :T] = (pb[a, :, 1, :T].astype(F32) + rb[a, 2, :, :T].astype(F32)).astype(BF)
        last_start(a, 1)

    def rs_final(a):
        rs_last(a, 0, 1).wait_recv()
        for p in (1, 2, 3, 7):
            for core in (0, 1):
                rs_last(a, BACK[p], core).wait_recv()
        for core in (0, 1):
            total = pb[a, :, 0, rows, :] if core == 0 else rbf[a, 0, 1]
            total = total.astype(F32)
            for slot in (1, 2, 3, 4):
                total = total + rbf[a, slot, core].astype(F32)
            rf[(mine if core == 0 else other) + a, 1] = total.astype(BF)
        for h in (a, 2 + a):
            for kv in (0, 1):
                pout[:, kv, h * D:(h + 1) * D] = rf[h, 1, kv]

    def place(a):
        return pl.ds(pl.multiple_of((2 * c + a) * (G * D), G * D), G * D)

    def o_copy(a):
        return remote(osend.at[a, 1], oout.at[:, place(a)], out_s.at[a, 0], out_r.at[a, 0], sib)

    def q_copy(a):
        return remote(qsend.at[a, 1], qout.at[:, place(a)], out_s.at[a, 1], out_r.at[a, 1], sib)

    def o_own(a):
        return pltpu.make_async_copy(osend.at[a, 0], oout.at[:, place(a)], own.at[a, 0])

    def q_own(a):
        return pltpu.make_async_copy(qsend.at[a, 0], qout.at[:, place(a)], own.at[a, 1])

    def r_copy(a):
        return remote(rsend.at[a], rf.at[2 * c + a, 0], out_s.at[a, 2], out_r.at[a, 2], sib)

    def at_step(i, hooks):
        for k, calls in hooks.items():
            @pl.when(i == k)
            def _():
                for call in calls:
                    call()

    def stacked(ref, a, b):
        return jnp.concatenate([ref[b, :, (a * G + g) * D:(a * G + g + 1) * D] for g in range(G)], axis=0)

    def queries_of(a):
        return jnp.concatenate([stacked(xq, a, 0), stacked(xq, a, 1)], axis=0)

    def fold(value, op):
        n = value.shape[0]
        return op(value.reshape(n // 8, 8, R), axis=0)

    def shard(a, kv, j):
        return kvb[a, kv, pl.ds(j * STEP, STEP)].reshape(N, D)

    def loop(hooks, works, ends=None):
        def step(i, _):
            at_step(i, hooks)
            for work in works:
                work(i)
            at_step(i, ends or {})
            return 0

        lax.fori_loop(0, HALF, step, 0)

    def scores(a, half):
        def work(i):
            s = dot(shard(a, 0, half * HALF + i), queries_of(a), 1, 1)
            sb[a, i] = s
            mb[a] = jnp.maximum(mb[a], fold(s, jnp.max))

        return work

    def weigh(a, half):
        def work(i):
            j = half * HALF + i
            e = jnp.exp2(sb[a, i] * SCALE2 - tp[a] * SCALE2)
            lb[a] += fold(e, jnp.sum)
            low = e.astype(BF)
            eb[a, j] = low
            ot[a] += dot(shard(a, 1, j), low, 0, 0)

        return work

    def own_scores(a):
        slot = lax.broadcasted_iota(jnp.int32, (T, G, T), 2).reshape(T, COLS)
        key = lax.broadcasted_iota(jnp.int32, (T, COLS), 0)
        for b in (0, 1):
            s = dot(xr[a, b, 0], stacked(xq, a, b), 1, 1)
            srb[a, :, b * COLS:(b + 1) * COLS] = jnp.where(key <= slot, s, MASKED)
        mb[a] = fold(srb[a], jnp.max)

    def own_weights(a):
        tp[a] = jnp.max(mb[a], axis=0, keepdims=True)
        er = jnp.exp2(srb[a] * SCALE2 - tp[a] * SCALE2)
        lb[a] = fold(er, jnp.sum)
        erb[a] = er.astype(BF)
        for b in (0, 1):
            cols = slice(b * COLS, (b + 1) * COLS)
            ot[a, :, cols] = dot(xr[a, b, 1], erb[a, :, cols], 0, 0)

    def grown(a):
        mb[a] = jnp.broadcast_to(tp[a], (8, R))

    def shrink_first(a):
        top = jnp.max(mb[a], axis=0, keepdims=True)
        shrink = jnp.exp2((tp[a] - top) * SCALE2)
        tp[a] = top
        fr[a] = shrink
        lb[a] = lb[a] * shrink
        ot[a] = ot[a] * shrink

    def rowwise(a):
        inv = 1.0 / jnp.sum(lb[a], axis=0, keepdims=True)
        for b in (0, 1):
            on = xl[b, 0:1, :].astype(F32) > 0.0
            for g in range(G):
                lo = b * COLS + g * T
                cols = slice(lo, lo + T)
                hd = slice((a * G + g) * D, (a * G + g + 1) * D)
                att = ot[a, :, cols] * inv[:, cols]
                gt = jnp.where(on, xg[b, :, hd].astype(F32).T, 0.0)
                delta = jnp.sum(gt * att, axis=0, keepdims=True) * inv[:, cols]
                gt = gt * inv[:, cols]
                shrink = fr[a, :, cols]
                dlt[a, 0, :, cols] = delta * shrink
                dlt[a, 1, :, cols] = delta
                gp[a, 0, cols, :] = (gt * shrink).T.astype(BF)
                gp[a, 1, cols, :] = gt.T.astype(BF)
                att = jnp.where(on, att, 0.0).T.astype(BF)
                osend[a, b, :, g * D:(g + 1) * D] = att
        o_copy(a).start()
        o_own(a).start()

    def backward(a, half):
        def work(i):
            j = HALF + i if half else HALF - 1 - i
            ps = pl.ds(j * STEP, STEP)
            scaled = gp[a, half]
            dp = dot(shard(a, 1, j), scaled, 1, 1) - dlt[a, half]
            ds = (eb[a, j].astype(F32) * dp).astype(BF)
            pb[a, 1, ps] = dot(eb[a, j], scaled, 1, 0).astype(BF).reshape(STEP, BLK, D)
            pb[a, 0, ps] = (dot(ds, queries_of(a), 1, 0) * INV_ROOT).astype(BF).reshape(STEP, BLK, D)
            dqt[a] += dot(shard(a, 0, j), ds, 0, 0)

        return work

    def backward_own(a):
        for b in (0, 1):
            cols = slice(b * COLS, (b + 1) * COLS)
            dp = dot(xr[a, b, 1], gp[a, 0, cols, :], 1, 1) - dlt[a, 0, :, cols]
            ds = (erb[a, :, cols].astype(F32) * dp).astype(BF)
            dv = dot(erb[a, :, cols], gp[a, 0, cols, :], 1, 0).astype(BF)
            dk = (dot(ds, stacked(xq, a, b), 1, 0) * INV_ROOT).astype(BF)
            dqt[a, :, cols] += dot(xr[a, b, 0], ds, 0, 0)
            if b == 0:
                rf[2 * c + a, 0, 0] = dk
                rf[2 * c + a, 0, 1] = dv
            else:
                rsend[a, 0] = dk
                rsend[a, 1] = dv
        r_copy(a).start()
        for b in (0, 1):
            for g in range(G):
                lo = b * COLS + g * T
                got = (dqt[a, :, lo:lo + T] * INV_ROOT).T.astype(BF)
                qsend[a, b, :, g * D:(g + 1) * D] = got
        q_copy(a).start()
        q_own(a).start()

    f = functools.partial

    def far_ends(a):
        return {0: [rs(a, 3).start, rs(a, 4).start], 1: [rs(a, 5).start, rs(a, 6).start, f(last_start, a, 7)]}

    def near_ends(a):
        return {0: [f(sum_three, a), f(sum_two, a)], 1: [f(sum_one, a), rs_last(a, 0, 1).start]}

    for pair in (ex_q, ex_r, ex_kv):
        exchange_wait(pair)
    for a in (0, 1):
        dqt[a] = jnp.zeros((D, R), F32)
    own_scores(0)
    loop({0: [f(ag_second, 0, 0)]}, [scores(0, 0)])
    own_weights(0)
    own_scores(1)
    loop({0: [f(ag_second, 0, 1), f(ag_second, 1, 0)]}, [weigh(0, 0), scores(1, 0)])
    own_weights(1)
    loop({0: [f(ag_second, 1, 1)], 1: [f(ag_third, 0, 0)]}, [weigh(1, 0)])
    grown(0)
    loop({0: [f(ag_wait, 0, 0, 3, 4)], 1: [f(ag_third, 0, 1), f(ag_wait, 0, 0, 7)]}, [scores(0, 1)])
    shrink_first(0)
    loop({0: [f(ag_wait, 0, 1, 3, 4)], 1: [f(ag_wait, 0, 1, 7)]}, [weigh(0, 1)])
    exchange_wait(ex_g)
    exchange_wait(ex_l)
    rowwise(0)
    loop({0: [f(ag_third, 1, 0)], 1: [f(ag_third, 1, 1)]}, [backward(0, 1)], far_ends(0))
    grown(1)
    loop({0: [f(ag_wait, 1, 0, 3, 4)], 1: [f(ag_wait, 1, 0, 7)]}, [scores(1, 1)])
    shrink_first(1)
    loop({0: [f(ag_wait, 1, 1, 3, 4)], 1: [f(ag_wait, 1, 1, 7)]}, [weigh(1, 1)])
    rowwise(1)
    loop({}, [backward(1, 1)], far_ends(1))
    loop({}, [backward(0, 0)], near_ends(0))
    loop({}, [backward(1, 0)], near_ends(1))
    backward_own(0)
    backward_own(1)
    rs_final(0)
    r_copy(0).wait()
    r_copy(1).wait()
    for h in range(KVH):
        for kv in (0, 1):
            rout[:, kv, h * D:(h + 1) * D] = rf[h, 0, kv]
    rs_final(1)

    for away, _ in (ex_q, ex_kv, ex_r, ex_g, ex_l):
        away.wait_send()
    for a in (0, 1):
        for kv in (0, 1):
            for p in near:
                direct(a, kv, p, 0).wait_send()
                direct(a, kv, p, 1).wait_send()
            for kind in range(3, 8):
                ag(a, kv, kind).wait_send()
        for kind in range(3, 7):
            rs(a, kind).wait_send()
        rs_last(a, 0, 1).wait_send()
        for p in (1, 2, 3, 7):
            rs_last(a, p, 0).wait_send()
            rs_last(a, p, 1).wait_send()
        o_copy(a).wait()
        q_copy(a).wait()
        o_own(a).wait()
        q_own(a).wait()


def hand_over(*refs):
    sources, targets, staged, sems = refs[:4], refs[4:8], refs[8:12], refs[12]
    arrive = [pltpu.make_async_copy(sources[k], staged[k], sems.at[0, k]) for k in range(4)]
    leave = [pltpu.make_async_copy(staged[k], targets[k], sems.at[1, k]) for k in range(4)]
    for copy in arrive:
        copy.start()
    for k in range(4):
        arrive[k].wait()
        leave[k].start()
    for copy in leave:
        copy.wait()


def per_device(prompt_kv, queries, response_key_values, grad_out, lengths):
    vmem = pl.BlockSpec(memory_space=pltpu.VMEM)
    anywhere = pl.BlockSpec(memory_space=pl.ANY)
    dma = pltpu.SemaphoreType.DMA
    flops = 6 * 2 * 2 * R * (NP * BLK + T) * D
    found = pl.pallas_call(
        kernel,
        out_shape=(
            jax.ShapeDtypeStruct(queries.shape, BF),
            jax.ShapeDtypeStruct(queries.shape, BF),
            jax.ShapeDtypeStruct(prompt_kv.shape, BF),
            jax.ShapeDtypeStruct(prompt_kv.shape, BF),
        ),
        in_specs=[pl.BlockSpec(memory_space=pltpu.SMEM), vmem, vmem, anywhere, anywhere],
        out_specs=(anywhere, anywhere, vmem, vmem),
        scratch_shapes=[
            pltpu.VMEM((KVH, 2, T, D), BF),
            pltpu.VMEM((KVH, 2, T, D), BF),
            pltpu.VMEM((16, T), BF),
            pltpu.VMEM((2, 2, NP, BLK, D), BF),
            pltpu.VMEM((2, T, 2 * G * D), BF),
            pltpu.VMEM((2, T, 2 * G * D), BF),
            pltpu.VMEM((2, 2, 2, T, D), BF),
            pltpu.VMEM((2, 16, T), BF),
            pltpu.VMEM((2, HALF, N, R), F32),
            pltpu.VMEM((2, T, R), F32),
            pltpu.VMEM((2, NI, N, R), BF),
            pltpu.VMEM((2, T, R), BF),
            pltpu.VMEM((2, 8, R), F32),
            pltpu.VMEM((2, 1, R), F32),
            pltpu.VMEM((2, 8, R), F32),
            pltpu.VMEM((2, D, R), F32),
            pltpu.VMEM((2, 1, R), F32),
            pltpu.VMEM((2, 2, R, D), BF),
            pltpu.VMEM((2, 2, 1, R), F32),
            pltpu.VMEM((2, D, R), F32),
            pltpu.VMEM((2, 2, T, G * D), BF),
            pltpu.VMEM((2, 2, T, G * D), BF),
            pltpu.VMEM((KVH, 2, 2, T, D), BF),
            pltpu.VMEM((2, 2, T, D), BF),
            pltpu.VMEM((2, 2, NP, BLK, D), BF),
            pltpu.VMEM((2, 4, 2, BLK, D), BF),
            pltpu.VMEM((2, 5, 2, 2, T, D), BF),
            dma((5,)), dma((5,)), dma((5,)),
            dma((2, 2, 4, 2)), dma((2, 2, 4, 2)),
            dma((2, 2, 5)), dma((2, 2, 5)),
            dma((2, 4)), dma((2, 4)),
            dma((2, 5, 2)), dma((2, 5, 2)),
            dma((2, 3)), dma((2, 3)), dma((2, 2)),
        ],
        compiler_params=pltpu.CompilerParams(
            collective_id=0, has_side_effects=True, vmem_limit_bytes=60 << 20),
        cost_estimate=pl.CostEstimate(flops=flops, bytes_accessed=8 << 20, transcendentals=2 * R * (NP * BLK + T)),
        name="shared_prompt_attention",
    )(lengths, prompt_kv, response_key_values, queries, grad_out)
    return pl.pallas_call(
        hand_over,
        out_shape=tuple(jax.ShapeDtypeStruct(v.shape, v.dtype) for v in found),
        in_specs=[anywhere] * 4,
        out_specs=(anywhere,) * 4,
        scratch_shapes=[pltpu.VMEM(v.shape, v.dtype) for v in found] + [dma((2, 4))],
        name="hand_over",
    )(*found)


def solution(mesh):
    wide, thick = P(("grp", "resp"), None), P(("grp", "resp"), None, None)
    return jax.shard_map(
        per_device,
        mesh=mesh,
        in_specs=(thick, wide, thick, wide, P(("grp", "resp"))),
        out_specs=(wide, wide, thick, thick),
        check_vma=False,
    )
```

```python
import functools
import math

import jax
import jax.numpy as jnp
from jax import lax
from jax.experimental import pallas as pl
from jax.experimental.pallas import tpu as pltpu
from jax.sharding import PartitionSpec as P

D = 128
T = 128
G = 5
KVH = 4
BLK = 2 * T
COLS = G * T
R = 2 * COLS
NP = 8
MASKED = -1e30
INV_ROOT = 1.0 / math.sqrt(D)
SCALE2 = INV_ROOT * math.log2(math.e)
BF = jnp.bfloat16
F32 = jnp.float32
MESH = pl.DeviceIdType.MESH


def dot(a, b, ca, cb):
    return lax.dot_general(a, b, (((ca,), (cb,)), ((), ())), preferred_element_type=F32)


STEP = 2
NI = NP // STEP
N = STEP * BLK
HALF = NI // 2
BACK = (0, 2, 1, 3, 5, 4, 6, 7)
LAST = {0: 0, 1: 1, 2: 2, 3: 3, 7: 4}


def kernel(lengths, prompt, resp, query, grad, oout, qout, rout, pout,
           pkv, rkv, live, kvb, xq, xg, xr, xl, sb, srb, eb, erb, mb, tp, lb, ot, fr, gp, dlt, dqt,
           osend, qsend, rf, rsend, pb, rb, rbf,
           st_s, st_r, loc, d_s, d_r, ag_s, ag_r, rs_s, rs_r, fin_s, fin_r, out_s, out_r, own):
    me = lax.axis_index("resp")
    z, x, c = me // 8, (me // 2) % 4, me % 2

    def device(p, core):
        dx = (0, 3, 1, 0, 3, 1, 2, 2)[p]
        zz = z if p in (0, 1, 2, 6) else 1 - z
        cc = c if core == 0 else 1 - c
        return zz * 8 + ((x + dx) % 4) * 2 + cc

    def remote(src, dst, ss, rs, to):
        return pltpu.make_async_remote_copy(
            src_ref=src, dst_ref=dst, send_sem=ss, recv_sem=rs, device_id={"resp": to}, device_id_type=MESH)

    barrier = pltpu.get_barrier_semaphore()
    peers = [(p, core) for p in (0, 1, 2, 3, 7) for core in (0, 1) if p or core]
    for p, core in peers:
        pl.semaphore_signal(barrier, inc=1, device_id={"resp": device(p, core)}, device_id_type=MESH)

    sib = device(0, 1)
    mine, other = 2 * c, 2 * (1 - c)
    rows = pl.ds(pl.multiple_of(c * T, T), T)
    orows = pl.ds(pl.multiple_of((1 - c) * T, T), T)
    W = 2 * G * D

    def columns(which):
        return pl.ds(pl.multiple_of(which * W, W), W)

    def by_head(src, dst):
        wide = src[...].astype(F32).reshape(T, 2, KVH * D).transpose(1, 0, 2).astype(BF)
        for h in range(KVH):
            for kv in (0, 1):
                dst[h, kv] = wide[kv, :, h * D:(h + 1) * D]

    by_head(prompt, pkv)
    live[...] = (lax.broadcasted_iota(jnp.int32, (16, T), 1) < lengths[0]).astype(F32).astype(BF)
    pl.semaphore_wait(barrier, len(peers))

    def direct(a, kv, p, core):
        head = (mine if core == 0 else other) + a
        return remote(pkv.at[head, kv], kvb.at[a, kv, BACK[p], rows, :],
                      d_s.at[a, kv, BACK[p], core], d_r.at[a, kv, BACK[p], core], device(p, core))

    near = (3, 1, 2)

    def direct_start(a, kv):
        for p in near:
            direct(a, kv, p, 0).start()
            direct(a, kv, p, 1).start()

    def exchange(k, src_other, src_mine, dst_other, dst_mine):
        away = remote(src_other, dst_other, st_s.at[k], st_r.at[k], sib)
        away.start()
        here = pltpu.make_async_copy(src_mine, dst_mine, loc.at[k])
        here.start()
        return away, here

    def exchange_wait(pair):
        pair[0].wait_recv()
        pair[1].wait()

    def heads_of(which):
        return pl.ds(which, 2)

    direct_start(0, 0)
    ex_q = exchange(0, query.at[:, columns(1 - c)], query.at[:, columns(c)], xq.at[1], xq.at[0])
    ex_kv = exchange(1, pkv.at[heads_of(other)], pkv.at[heads_of(mine)],
                     kvb.at[:, :, 0, rows, :], kvb.at[:, :, 0, rows, :])
    direct_start(0, 1)
    direct_start(1, 0)
    direct_start(1, 1)
    by_head(resp, rkv)
    ex_r = exchange(2, rkv.at[heads_of(other)], rkv.at[heads_of(mine)], xr.at[:, 1], xr.at[:, 0])
    ex_g = exchange(3, grad.at[:, columns(1 - c)], grad.at[:, columns(c)], xg.at[1], xg.at[0])
    ex_l = exchange(4, live, live, xl.at[1], xl.at[0])

    def ag(a, kv, kind):
        to = {3: 2, 4: 1, 5: 2, 6: 1, 7: 3}[kind]
        src = {3: 3, 4: 3, 5: 1, 6: 2, 7: 6}[kind]
        dst = {3: 4, 4: 5, 5: 6, 6: 6, 7: 7}[kind]
        part = {5: pl.ds(0, T), 6: pl.ds(T, T)}.get(kind, pl.ds(0, BLK))
        return remote(kvb.at[a, kv, src, part, :], kvb.at[a, kv, dst, part, :],
                      ag_s.at[a, kv, kind - 3], ag_r.at[a, kv, kind - 3], device(to, 0))

    def ag_second(a, kv):
        for p in near:
            direct(a, kv, BACK[p], 0).wait_recv()
            direct(a, kv, BACK[p], 1).wait_recv()
        for k in (5, 6, 3, 4):
            ag(a, kv, k).start()

    def ag_third(a, kv):
        ag(a, kv, 5).wait_recv()
        ag(a, kv, 6).wait_recv()
        ag(a, kv, 7).start()

    def ag_wait(a, kv, *kinds):
        for k in kinds:
            ag(a, kv, k).wait_recv()

    def rs(a, kind):
        to = {3: 1, 4: 2, 5: 1, 6: 2}[kind]
        src = {3: 4, 4: 5, 5: 6, 6: 6}[kind]
        part = {5: pl.ds(0, T), 6: pl.ds(T, T)}.get(kind, pl.ds(0, BLK))
        return remote(pb.at[a, :, src, part, :], rb.at[a, kind - 3, :, part, :],
                      rs_s.at[a, kind - 3], rs_r.at[a, kind - 3], device(to, 0))

    def rs_last(a, p, core):
        slot = LAST[BACK[p]]
        return remote(pb.at[a, :, p, rows if core == 0 else orows, :], rbf.at[a, slot, core],
                      fin_s.at[a, slot, core], fin_r.at[a, slot, core], device(p, core))

    def last_start(a, p):
        rs_last(a, p, 0).start()
        rs_last(a, p, 1).start()

    def sum_three(a):
        rs(a, 3).wait_recv()
        rs(a, 4).wait_recv()
        pb[a, :, 3] = (pb[a, :, 3].astype(F32) + rb[a, 0].astype(F32) + rb[a, 1].astype(F32)).astype(BF)
        last_start(a, 3)

    def sum_two(a):
        rs(a, 6).wait_recv()
        pb[a, :, 2, T:] = (pb[a, :, 2, T:].astype(F32) + rb[a, 3, :, T:].astype(F32)).astype(BF)
        last_start(a, 2)

    def sum_one(a):
        rs(a, 5).wait_recv()
        pb[a, :, 1, :T] = (pb[a, :, 1, :T].astype(F32) + rb[a, 2, :, :T].astype(F32)).astype(BF)
        last_start(a, 1)

    def rs_final(a):
        rs_last(a, 0, 1).wait_recv()
        for p in (1, 2, 3, 7):
            for core in (0, 1):
                rs_last(a, BACK[p], core).wait_recv()
        for core in (0, 1):
            total = pb[a, :, 0, rows, :] if core == 0 else rbf[a, 0, 1]
            total = total.astype(F32)
            for slot in (1, 2, 3, 4):
                total = total + rbf[a, slot, core].astype(F32)
            rf[(mine if core == 0 else other) + a, 1] = total.astype(BF)
        for h in (a, 2 + a):
            for kv in (0, 1):
                pout[:, kv, h * D:(h + 1) * D] = rf[h, 1, kv]

    def place(a):
        return pl.ds(pl.multiple_of((2 * c + a) * (G * D), G * D), G * D)

    def o_copy(a):
        return remote(osend.at[a, 1], oout.at[:, place(a)], out_s.at[a, 0], out_r.at[a, 0], sib)

    def q_copy(a):
        return remote(qsend.at[a, 1], qout.at[:, place(a)], out_s.at[a, 1], out_r.at[a, 1], sib)

    def o_own(a):
        return pltpu.make_async_copy(osend.at[a, 0], oout.at[:, place(a)], own.at[a, 0])

    def q_own(a):
        return pltpu.make_async_copy(qsend.at[a, 0], qout.at[:, place(a)], own.at[a, 1])

    def r_copy(a):
        return remote(rsend.at[a], rf.at[2 * c + a, 0], out_s.at[a, 2], out_r.at[a, 2], sib)

    def at_step(i, hooks):
        for k, calls in hooks.items():
            @pl.when(i == k)
            def _():
                for call in calls:
                    call()

    def stacked(ref, a, b):
        return jnp.concatenate([ref[b, :, (a * G + g) * D:(a * G + g + 1) * D] for g in range(G)], axis=0)

    def queries_of(a):
        return jnp.concatenate([stacked(xq, a, 0), stacked(xq, a, 1)], axis=0)

    def fold(value, op):
        n = value.shape[0]
        return op(value.reshape(n // 8, 8, R), axis=0)

    def shard(a, kv, j):
        return kvb[a, kv, pl.ds(j * STEP, STEP)].reshape(N, D)

    def loop(hooks, works, ends=None):
        def step(i, _):
            at_step(i, hooks)
            for work in works:
                work(i)
            at_step(i, ends or {})
            return 0

        lax.fori_loop(0, HALF, step, 0)

    def scores(a, half):
        def work(i):
            s = dot(shard(a, 0, half * HALF + i), queries_of(a), 1, 1)
            sb[a, i] = s
            mb[a] = jnp.maximum(mb[a], fold(s, jnp.max))

        return work

    def weigh(a, half):
        def work(i):
            j = half * HALF + i
            e = jnp.exp2(sb[a, i] * SCALE2 - tp[a] * SCALE2)
            lb[a] += fold(e, jnp.sum)
            low = e.astype(BF)
            eb[a, j] = low
            ot[a] += dot(shard(a, 1, j), low, 0, 0)

        return work

    def own_scores(a):
        slot = lax.broadcasted_iota(jnp.int32, (T, G, T), 2).reshape(T, COLS)
        key = lax.broadcasted_iota(jnp.int32, (T, COLS), 0)
        for b in (0, 1):
            s = dot(xr[a, b, 0], stacked(xq, a, b), 1, 1)
            srb[a, :, b * COLS:(b + 1) * COLS] = jnp.where(key <= slot, s, MASKED)
        mb[a] = jnp.maximum(mb[a], fold(srb[a], jnp.max))

    def own_weights(a):
        tp[a] = jnp.max(mb[a], axis=0, keepdims=True)
        er = jnp.exp2(srb[a] * SCALE2 - tp[a] * SCALE2)
        lb[a] = fold(er, jnp.sum)
        erb[a] = er.astype(BF)
        for b in (0, 1):
            cols = slice(b * COLS, (b + 1) * COLS)
            ot[a, :, cols] = dot(xr[a, b, 1], erb[a, :, cols], 0, 0)

    def grown(a):
        mb[a] = jnp.broadcast_to(tp[a], (8, R))

    def shrink_first(a):
        top = jnp.max(mb[a], axis=0, keepdims=True)
        shrink = jnp.exp2((tp[a] - top) * SCALE2)
        tp[a] = top
        fr[a] = shrink
        lb[a] = lb[a] * shrink
        ot[a] = ot[a] * shrink

    def rowwise(a):
        inv = 1.0 / jnp.sum(lb[a], axis=0, keepdims=True)
        for b in (0, 1):
            on = xl[b, 0:1, :].astype(F32) > 0.0
            for g in range(G):
                lo = b * COLS + g * T
                cols = slice(lo, lo + T)
                hd = slice((a * G + g) * D, (a * G + g + 1) * D)
                att = ot[a, :, cols] * inv[:, cols]
                gt = jnp.where(on, xg[b, :, hd].astype(F32).T, 0.0)
                delta = jnp.sum(gt * att, axis=0, keepdims=True) * inv[:, cols]
                gt = gt * inv[:, cols]
                shrink = fr[a, :, cols]
                dlt[a, 0, :, cols] = delta * shrink
                dlt[a, 1, :, cols] = delta
                gp[a, 0, cols, :] = (gt * shrink).T.astype(BF)
                gp[a, 1, cols, :] = gt.T.astype(BF)
                att = jnp.where(on, att, 0.0).T.astype(BF)
                osend[a, b, :, g * D:(g + 1) * D] = att
        o_copy(a).start()
        o_own(a).start()

    def backward(a, half):
        def work(i):
            j = HALF + i if half else HALF - 1 - i
            ps = pl.ds(j * STEP, STEP)
            scaled = gp[a, half]
            dp = dot(shard(a, 1, j), scaled, 1, 1) - dlt[a, half]
            ds = (eb[a, j].astype(F32) * dp).astype(BF)
            pb[a, 1, ps] = dot(eb[a, j], scaled, 1, 0).astype(BF).reshape(STEP, BLK, D)
            pb[a, 0, ps] = (dot(ds, queries_of(a), 1, 0) * INV_ROOT).astype(BF).reshape(STEP, BLK, D)
            dqt[a] += dot(shard(a, 0, j), ds, 0, 0)

        return work

    def backward_own(a):
        for b in (0, 1):
            cols = slice(b * COLS, (b + 1) * COLS)
            dp = dot(xr[a, b, 1], gp[a, 0, cols, :], 1, 1) - dlt[a, 0, :, cols]
            ds = (erb[a, :, cols].astype(F32) * dp).astype(BF)
            dv = dot(erb[a, :, cols], gp[a, 0, cols, :], 1, 0).astype(BF)
            dk = (dot(ds, stacked(xq, a, b), 1, 0) * INV_ROOT).astype(BF)
            dqt[a, :, cols] += dot(xr[a, b, 0], ds, 0, 0)
            if b == 0:
                rf[2 * c + a, 0, 0] = dk
                rf[2 * c + a, 0, 1] = dv
            else:
                rsend[a, 0] = dk
                rsend[a, 1] = dv
        r_copy(a).start()
        for b in (0, 1):
            for g in range(G):
                lo = b * COLS + g * T
                got = (dqt[a, :, lo:lo + T] * INV_ROOT).T.astype(BF)
                qsend[a, b, :, g * D:(g + 1) * D] = got
        q_copy(a).start()
        q_own(a).start()

    f = functools.partial

    def far_ends(a):
        return {0: [rs(a, 3).start, rs(a, 4).start], 1: [rs(a, 5).start, rs(a, 6).start, f(last_start, a, 7)]}

    def near_ends(a):
        return {0: [f(sum_three, a), f(sum_two, a)], 1: [f(sum_one, a), rs_last(a, 0, 1).start]}

    exchange_wait(ex_q)
    exchange_wait(ex_kv)
    for a in (0, 1):
        dqt[a] = jnp.zeros((D, R), F32)
        mb[a] = jnp.full((8, R), MASKED, F32)
    loop({0: [f(ag_second, 0, 0)]}, [scores(0, 0)])
    exchange_wait(ex_r)
    own_scores(0)
    own_weights(0)
    own_scores(1)
    loop({0: [f(ag_second, 0, 1), f(ag_second, 1, 0)]}, [weigh(0, 0), scores(1, 0)])
    own_weights(1)
    loop({0: [f(ag_second, 1, 1)], 1: [f(ag_third, 0, 0)]}, [weigh(1, 0)])
    grown(0)
    loop({0: [f(ag_wait, 0, 0, 3, 4)], 1: [f(ag_third, 0, 1), f(ag_wait, 0, 0, 7)]}, [scores(0, 1)])
    shrink_first(0)
    loop({0: [f(ag_wait, 0, 1, 3, 4)], 1: [f(ag_wait, 0, 1, 7)]}, [weigh(0, 1)])
    exchange_wait(ex_g)
    exchange_wait(ex_l)
    rowwise(0)
    loop({0: [f(ag_third, 1, 0)], 1: [f(ag_third, 1, 1)]}, [backward(0, 1)], far_ends(0))
    grown(1)
    loop({0: [f(ag_wait, 1, 0, 3, 4)], 1: [f(ag_wait, 1, 0, 7)]}, [scores(1, 1)])
    shrink_first(1)
    loop({0: [f(ag_wait, 1, 1, 3, 4)], 1: [f(ag_wait, 1, 1, 7)]}, [weigh(1, 1)])
    rowwise(1)
    loop({}, [backward(1, 1)], far_ends(1))
    loop({}, [backward(0, 0)], near_ends(0))
    loop({}, [backward(1, 0)], near_ends(1))
    backward_own(0)
    backward_own(1)
    rs_final(0)
    r_copy(0).wait()
    r_copy(1).wait()
    for h in range(KVH):
        for kv in (0, 1):
            rout[:, kv, h * D:(h + 1) * D] = rf[h, 0, kv]
    rs_final(1)

    for away, _ in (ex_q, ex_kv, ex_r, ex_g, ex_l):
        away.wait_send()
    for a in (0, 1):
        for kv in (0, 1):
            for p in near:
                direct(a, kv, p, 0).wait_send()
                direct(a, kv, p, 1).wait_send()
            for kind in range(3, 8):
                ag(a, kv, kind).wait_send()
        for kind in range(3, 7):
            rs(a, kind).wait_send()
        rs_last(a, 0, 1).wait_send()
        for p in (1, 2, 3, 7):
            rs_last(a, p, 0).wait_send()
            rs_last(a, p, 1).wait_send()
        o_copy(a).wait()
        q_copy(a).wait()
        o_own(a).wait()
        q_own(a).wait()


def hand_over(*refs):
    sources, targets, staged, sems = refs[:4], refs[4:8], refs[8:12], refs[12]
    arrive = [pltpu.make_async_copy(sources[k], staged[k], sems.at[0, k]) for k in range(4)]
    leave = [pltpu.make_async_copy(staged[k], targets[k], sems.at[1, k]) for k in range(4)]
    for copy in arrive:
        copy.start()
    for k in range(4):
        arrive[k].wait()
        leave[k].start()
    for copy in leave:
        copy.wait()


def per_device(prompt_kv, queries, response_key_values, grad_out, lengths):
    vmem = pl.BlockSpec(memory_space=pltpu.VMEM)
    anywhere = pl.BlockSpec(memory_space=pl.ANY)
    dma = pltpu.SemaphoreType.DMA
    flops = 6 * 2 * 2 * R * (NP * BLK + T) * D
    found = pl.pallas_call(
        kernel,
        out_shape=(
            jax.ShapeDtypeStruct(queries.shape, BF),
            jax.ShapeDtypeStruct(queries.shape, BF),
            jax.ShapeDtypeStruct(prompt_kv.shape, BF),
            jax.ShapeDtypeStruct(prompt_kv.shape, BF),
        ),
        in_specs=[pl.BlockSpec(memory_space=pltpu.SMEM), vmem, vmem, anywhere, anywhere],
        out_specs=(anywhere, anywhere, vmem, vmem),
        scratch_shapes=[
            pltpu.VMEM((KVH, 2, T, D), BF),
            pltpu.VMEM((KVH, 2, T, D), BF),
            pltpu.VMEM((16, T), BF),
            pltpu.VMEM((2, 2, NP, BLK, D), BF),
            pltpu.VMEM((2, T, 2 * G * D), BF),
            pltpu.VMEM((2, T, 2 * G * D), BF),
            pltpu.VMEM((2, 2, 2, T, D), BF),
            pltpu.VMEM((2, 16, T), BF),
            pltpu.VMEM((2, HALF, N, R), F32),
            pltpu.VMEM((2, T, R), F32),
            pltpu.VMEM((2, NI, N, R), BF),
            pltpu.VMEM((2, T, R), BF),
            pltpu.VMEM((2, 8, R), F32),
            pltpu.VMEM((2, 1, R), F32),
            pltpu.VMEM((2, 8, R), F32),
            pltpu.VMEM((2, D, R), F32),
            pltpu.VMEM((2, 1, R), F32),
            pltpu.VMEM((2, 2, R, D), BF),
            pltpu.VMEM((2, 2, 1, R), F32),
            pltpu.VMEM((2, D, R), F32),
            pltpu.VMEM((2, 2, T, G * D), BF),
            pltpu.VMEM((2, 2, T, G * D), BF),
            pltpu.VMEM((KVH, 2, 2, T, D), BF),
            pltpu.VMEM((2, 2, T, D), BF),
            pltpu.VMEM((2, 2, NP, BLK, D), BF),
            pltpu.VMEM((2, 4, 2, BLK, D), BF),
            pltpu.VMEM((2, 5, 2, 2, T, D), BF),
            dma((5,)), dma((5,)), dma((5,)),
            dma((2, 2, 4, 2)), dma((2, 2, 4, 2)),
            dma((2, 2, 5)), dma((2, 2, 5)),
            dma((2, 4)), dma((2, 4)),
            dma((2, 5, 2)), dma((2, 5, 2)),
            dma((2, 3)), dma((2, 3)), dma((2, 2)),
        ],
        compiler_params=pltpu.CompilerParams(
            collective_id=0, has_side_effects=True, vmem_limit_bytes=60 << 20),
        cost_estimate=pl.CostEstimate(flops=flops, bytes_accessed=8 << 20, transcendentals=2 * R * (NP * BLK + T)),
        name="shared_prompt_attention",
    )(lengths, prompt_kv, response_key_values, queries, grad_out)
    return pl.pallas_call(
        hand_over,
        out_shape=tuple(jax.ShapeDtypeStruct(v.shape, v.dtype) for v in found),
        in_specs=[anywhere] * 4,
        out_specs=(anywhere,) * 4,
        scratch_shapes=[pltpu.VMEM(v.shape, v.dtype) for v in found] + [dma((2, 4))],
        name="hand_over",
    )(*found)


def solution(mesh):
    wide, thick = P(("grp", "resp"), None), P(("grp", "resp"), None, None)
    return jax.shard_map(
        per_device,
        mesh=mesh,
        in_specs=(thick, wide, thick, wide, P(("grp", "resp"))),
        out_specs=(wide, wide, thick, thick),
        check_vma=False,
    )
```
